512 devices in a mesh: seq: 64 (over z, x), head: 8 (over y, core).
Axes of the slice: x: 4, y: 4, z: 16, core: 2. Of those that a mesh axis runs over, the one named last changes fastest.
Arguments:
- delta_query: bfloat16 [16384, 32, 128], P('seq', 'head'), may hold values from -40 to 40
- delta_key: bfloat16 [16384, 32, 128], P('seq', 'head'), may hold values from -40 to 40
- delta_value: bfloat16 [16384, 32, 256], P('seq', 'head'), may hold values from -16 to 16
- delta_gate: float32 [16384, 32], P('seq', 'head'), may hold values from -1 to 0
- delta_beta: float32 [16384, 32], P('seq', 'head'), may hold values from 0 to 1
- delta_count: int32 [64], P('seq'), may hold values from 32 to 256, as said below
- delta_gain: float32 [32, 256], P('head'), may hold values from 0.1 to 1.9
- attn_query: bfloat16 [16384, 32, 128], P('seq', 'head'), may hold values from -6 to 6
- attn_key: bfloat16 [16384, 32, 128], P('seq', 'head'), may hold values from -6 to 6
- attn_value: bfloat16 [16384, 32, 256], P('seq', 'head'), may hold values from -6 to 6
- attn_position: int32 [16384], P('seq'), may hold values from 0 to 32767, as said below
- attn_count: int32 [64], P('seq'), may hold values from 32 to 256, as said below
Outputs:
- delta_out: bfloat16 [16384, 32, 256], P('seq', 'head')
- attn_out: bfloat16 [16384, 32, 256], P('seq', 'head')
The draws below stay inside these ranges and needn't reach their ends.
Inputs may be any that keep to these rules, and one draw needn't show every extreme that they name: `delta_count`: kept rows of each block of 512 token positions; some block holds exactly 256. `attn_count`: kept rows of each block of 512 token positions; some block holds exactly 256. `attn_position`: slot s holds a position of block b = s // 256, from b * 512 to (b + 1) * 512 - 1; the first attn_count[b] slots of a block hold distinct positions in rising order, its other slots arbitrary positions of the block.
All inputs are finite; a program needn't handle non-finite values.
Results may differ from the reference program's by a relative error of at most 0.0044.
Values may be sent and summed in bfloat16 or wider, within the bound.
No kernel may reach another device: no remote copies, remote signals or barrier semaphores. Data moves between devices by JAX's collectives and lax.ppermute only.
A program may use at most 128 MiB of HBM per device.

```python
import math
import jax
import jax.numpy as jnp
from jax import lax

H = 32
KD = 128
VD = 256
WINDOW = 2048
GROUP = 64
TOK_DEV = 512
KEPT_ROW_SLOTS = 256
SLOTS = 16384
N_SEQ = 64


def block_counts(seed_key):
    lowest = max(3, KEPT_ROW_SLOTS // 8)
    first_key, second_key = jax.random.split(seed_key)
    raw_draws = jax.random.randint(first_key, (N_SEQ,), 0, 64)
    counts = lowest + (KEPT_ROW_SLOTS - lowest) * raw_draws * raw_draws // 3969
    full_block = jax.random.randint(second_key, (), 0, N_SEQ)
    return counts.at[full_block].set(KEPT_ROW_SLOTS).astype(jnp.int32)


def shuffle_block(block_key):
    return jax.random.permutation(block_key, TOK_DEV)


def attention_kept(seed_key):
    seed_key = jax.random.fold_in(seed_key, 23)
    counts = block_counts(jax.random.fold_in(seed_key, 1))
    block_keys = jax.random.split(jax.random.fold_in(seed_key, 2), N_SEQ)
    orders = jax.vmap(shuffle_block)(block_keys)
    block_ids = jnp.arange(N_SEQ)[:, None]
    target = jnp.where(block_ids == 0, 0, jnp.where(block_ids == N_SEQ - 1, TOK_DEV - 1, -1))
    column_ids = jnp.arange(TOK_DEV)[None, :]
    first_entry = orders[:, 0:1]
    orders = jnp.where((target >= 0) & (orders == target), first_entry, orders)
    orders = jnp.where((target >= 0) & (column_ids == 0), target, orders)
    slot_index = jnp.arange(TOK_DEV)[None, :]
    chosen = jnp.where(slot_index < counts[:, None], orders, TOK_DEV)
    ordered = jnp.sort(chosen, axis=1)[:, :KEPT_ROW_SLOTS]
    filler = jax.random.randint(jax.random.fold_in(seed_key, 3), (N_SEQ, KEPT_ROW_SLOTS), 0, TOK_DEV)
    local_spot = jnp.where(ordered < TOK_DEV, ordered, filler)
    block_start = (jnp.arange(N_SEQ) * TOK_DEV)[:, None]
    return (counts, (block_start + local_spot).reshape(-1).astype(jnp.int32))


def draw_delta_count(key, part):
    key = jax.random.fold_in(key, 11)
    return block_counts(key)


def draw_attn_count(key, part):
    counts, positions = attention_kept(key)
    return counts


def draw_attn_position(key, part):
    counts, positions = attention_kept(key)
    return positions


def loguniform(seed_key, shape, lowest, highest):
    return jnp.exp(jax.random.uniform(seed_key, shape, jnp.float32, math.log(lowest), math.log(highest)))


def slow_heads(seed_key, slow_share):
    return jax.random.uniform(jax.random.fold_in(seed_key, 5), (H,)) < slow_share


def draw_delta_gate(key, part):
    slow_mask = slow_heads(key, 0.5)
    key = jax.random.fold_in(key, 53)
    every_key_row = jax.random.split(key, 6)
    sequence_length = N_SEQ * KEPT_ROW_SLOTS
    slow_rate = loguniform(every_key_row[0], (H,), 0.1, 1.0) * 0.7 / sequence_length
    fast_rate = loguniform(every_key_row[1], (H,), 1.0 / 50.0, 1.0 / 30.0)
    rate_head = jnp.where(slow_mask, slow_rate, fast_rate)
    block_factor = loguniform(every_key_row[2], (N_SEQ, 1, H), 0.5, 2.0)
    row_factor = jax.random.uniform(every_key_row[3], (N_SEQ, KEPT_ROW_SLOTS, H), jnp.float32, 0.5, 1.5)
    gate_amount = -(rate_head * block_factor * row_factor)
    dropped_clusters = jax.random.uniform(every_key_row[4], (N_SEQ, KEPT_ROW_SLOTS, 1)) < 8.0 / sequence_length
    cluster_dropout = jnp.log(jax.random.uniform(every_key_row[5], (N_SEQ, KEPT_ROW_SLOTS, 1), jnp.float32, 0.5, 0.8))
    gate_amount = jnp.where(dropped_clusters, gate_amount + cluster_dropout, gate_amount)
    return gate_amount.reshape(N_SEQ * KEPT_ROW_SLOTS, H)


def draw_delta_beta(key, part):
    slow_mask = slow_heads(key, 0.5)
    key = jax.random.fold_in(key, 61)
    first_key, second_key, third_key = jax.random.split(key, 3)
    small_scale = loguniform(first_key, (H,), 0.003, 0.02)
    large_scale = loguniform(second_key, (H,), 0.1, 1.0)
    head_scale = jnp.where(slow_mask, small_scale, large_scale)
    row_factor = jax.random.uniform(third_key, (N_SEQ * KEPT_ROW_SLOTS, H), jnp.float32, 0.5, 1.0)
    return head_scale * row_factor


def draw_delta_query(key, part):
    key = jax.random.fold_in(key, 41)
    first_key, second_key = jax.random.split(key, 2)
    row_scale = loguniform(first_key, (N_SEQ * KEPT_ROW_SLOTS, H, 1), 1.0, 10.0)
    noise_part = jnp.clip(jax.random.normal(second_key, (N_SEQ * KEPT_ROW_SLOTS, H, KD), jnp.float32), -4.0, 4.0)
    return (noise_part * row_scale).astype(jnp.bfloat16)


def draw_delta_key(key, part):
    key = jax.random.fold_in(key, 43)
    first_key, second_key = jax.random.split(key, 2)
    row_scale = loguniform(first_key, (N_SEQ * KEPT_ROW_SLOTS, H, 1), 1.0, 10.0)
    noise_part = jnp.clip(jax.random.normal(second_key, (N_SEQ * KEPT_ROW_SLOTS, H, KD), jnp.float32), -4.0, 4.0)
    return (noise_part * row_scale).astype(jnp.bfloat16)


def draw_delta_value(key, part):
    key = jax.random.fold_in(key, 71)
    ladder = jnp.arange(H, dtype=jnp.float32) / (H - 1)
    noise_part = jnp.clip(jax.random.normal(key, (N_SEQ * KEPT_ROW_SLOTS, H, VD), jnp.float32), -4.0, 4.0)
    return (noise_part * (3.0 ** ladder)[None, :, None]).astype(jnp.bfloat16)


def draw_attn_query(key, part):
    key = jax.random.fold_in(key, 31)
    return jnp.clip(jax.random.normal(key, (N_SEQ * KEPT_ROW_SLOTS, H, KD), jnp.float32), -6.0, 6.0).astype(jnp.bfloat16)


def draw_attn_key(key, part):
    key = jax.random.fold_in(key, 37)
    return jnp.clip(jax.random.normal(key, (N_SEQ * KEPT_ROW_SLOTS, H, KD), jnp.float32), -6.0, 6.0).astype(jnp.bfloat16)


def levels(own_key, extent, shards, least, high):
    level, own = 1.0, jax.random.fold_in(own_key, 6)
    for dim, parts in shards:
        steps = jnp.exp(jax.random.uniform(jax.random.fold_in(own, dim), (parts,), jnp.float32, least / len(shards), high / len(shards)))
        level = level * jnp.repeat(steps, extent[dim] // parts).reshape([-1 if axis == dim else 1 for axis in range(len(extent))])
    return level


def scatter_about(key, shape, deviation, reach, pieces=(), kind=jnp.bfloat16):
    values = jax.random.normal(key, shape, jnp.float32) * deviation
    if len(pieces) > 0:
        values = levels(key, shape, pieces, -0.22, 0.18) * values
    return jnp.clip(values, min=-reach, max=reach).astype(kind)


def setup_inputs(seed: int = 0) -> dict:
    arg_keys = jax.random.split(jax.random.key(seed), 13)
    return {
        "delta_query": draw_delta_query(jax.random.fold_in(arg_keys[12], 71), 0),
        "delta_key": draw_delta_key(jax.random.fold_in(arg_keys[12], 71), 0),
        "delta_value": draw_delta_value(jax.random.fold_in(arg_keys[12], 71), 0),
        "delta_gate": draw_delta_gate(jax.random.fold_in(arg_keys[12], 71), 0),
        "delta_beta": draw_delta_beta(jax.random.fold_in(arg_keys[12], 71), 0),
        "delta_count": draw_delta_count(jax.random.fold_in(arg_keys[12], 71), 0),
        "delta_gain": jnp.clip(1.0 + 0.18 * jax.random.normal(arg_keys[6], (H, VD), jnp.float32), 0.1, 1.9),
        "attn_query": draw_attn_query(jax.random.fold_in(arg_keys[12], 71), 0),
        "attn_key": draw_attn_key(jax.random.fold_in(arg_keys[12], 71), 0),
        "attn_value": scatter_about(arg_keys[9], (SLOTS, H, VD), 1.0, 6.0, ((0, 64), (1, 8))),
        "attn_position": draw_attn_position(jax.random.fold_in(arg_keys[12], 71), 0),
        "attn_count": draw_attn_count(jax.random.fold_in(arg_keys[12], 71), 0),
    }


HIGHEST = lax.Precision.HIGHEST

def inverse_norms(block_rows):
    wide_rows = block_rows.astype(jnp.float32)
    return lax.rsqrt(lax.optimization_barrier(jnp.sum(wide_rows * wide_rows, axis=-1)) + 1e-06)

def group_terms(query_raw, key_raw, value_rows, gate_rows, beta_rows):
    group_len = gate_rows.shape[0]
    row_index = jnp.arange(group_len)[:, None]
    col_index = jnp.arange(group_len)[None, :]
    query_scale = inverse_norms(query_raw)
    key_scale = inverse_norms(key_raw)
    query_rows = query_raw.astype(jnp.float32) * query_scale[:, None]
    key_rows = key_raw.astype(jnp.float32) * key_scale[:, None]
    log_decay = jnp.cumsum(gate_rows)
    decay_pair = jnp.where(col_index <= row_index, jnp.exp(jnp.minimum(log_decay[:, None] - log_decay[None, :], 0.0)), 0.0)
    key_gram = key_scale[:, None] * jnp.dot(key_raw.astype(jnp.float32), key_raw.T.astype(jnp.float32), preferred_element_type=jnp.float32) * key_scale[None, :]
    system = jnp.eye(group_len, dtype=jnp.float32) + jnp.where(col_index < row_index, beta_rows[:, None] * decay_pair * key_gram, 0.0)
    decay_to = jnp.exp(log_decay)
    right_side = jnp.concatenate([beta_rows[:, None] * value_rows, (beta_rows * decay_to)[:, None] * key_rows], axis=1)
    solved = lax.linalg.triangular_solve(system, right_side, left_side=True, lower=True)
    value_width = value_rows.shape[1]
    new_value = solved[:, :value_width]
    new_key = solved[:, value_width:]
    query_key = query_scale[:, None] * jnp.dot(query_raw.astype(jnp.float32), key_raw.T.astype(jnp.float32), preferred_element_type=jnp.float32) * key_scale[None, :]
    mixing = decay_pair * query_key
    decay_tail = jnp.exp(log_decay[-1] - log_decay)[:, None]
    local_out = jnp.dot(mixing, new_value, precision=HIGHEST)
    carry_out = decay_to[:, None] * query_rows - jnp.dot(mixing, new_key, precision=HIGHEST)
    transition = decay_to[-1] * jnp.eye(key_rows.shape[1], dtype=jnp.float32) - jnp.dot(key_rows.T, decay_tail * new_key, precision=HIGHEST)
    offset = jnp.dot(key_rows.T, decay_tail * new_value, precision=HIGHEST)
    return (local_out, carry_out, transition, offset)

def head_run(inputs):
    query_rows, key_rows, value_rows, gate_rows, beta_rows = inputs

    def advance(state_now, items):
        local_out, carry_out, transition, offset = group_terms(*items)
        result = local_out + jnp.dot(carry_out, state_now, precision=HIGHEST)
        return (jnp.dot(transition, state_now, precision=HIGHEST) + offset, result)
    start_state = jnp.zeros((key_rows.shape[2], value_rows.shape[2]), jnp.float32)
    _, outcome = lax.scan(advance, start_state, (query_rows, key_rows, value_rows, gate_rows, beta_rows))
    return outcome

def window_attend(query_rows, query_marks, key_rows, value_rows, key_marks):
    score_scale = query_rows.shape[2] ** (-0.5)
    scores = jnp.einsum('qhd,khd->hqk', query_rows.astype(jnp.float32), key_rows.astype(jnp.float32)) * score_scale
    permitted_pairs = (key_marks[None, :] > 0) & (key_marks[None, :] <= query_marks[:, None]) & (key_marks[None, :] > query_marks[:, None] - WINDOW)
    scores = jnp.where(permitted_pairs[None], scores, -1e+30)
    top_score = lax.optimization_barrier(jnp.max(scores, axis=2, keepdims=True))
    weights = jnp.exp(scores - top_score)
    totals = lax.optimization_barrier(jnp.sum(weights, axis=2))
    rounded = weights.astype(jnp.bfloat16)
    mixed_rows = jnp.einsum('hqk,khv->qhv', rounded.astype(jnp.float32), value_rows.astype(jnp.float32))
    mixed_rows = mixed_rows / jnp.transpose(totals)[:, :, None]
    return jnp.where((query_marks > 0)[:, None, None], mixed_rows, 0.0).astype(jnp.bfloat16)

def reference(delta_query, delta_key, delta_value, delta_gate, delta_beta, delta_count, delta_gain, attn_query, attn_key, attn_value, attn_position, attn_count):
    slot_total = delta_gate.shape[0]
    slot_in_block = jnp.arange(slot_total, dtype=jnp.int32) % KEPT_ROW_SLOTS
    live_delta = slot_in_block < jnp.repeat(delta_count, KEPT_ROW_SLOTS, total_repeat_length=slot_total)
    gate_live = jnp.where(live_delta[:, None], delta_gate, 0.0)
    beta_live = jnp.where(live_delta[:, None], delta_beta, 0.0)
    blocks = slot_total // GROUP

    def arrange(array):
        moved_axes = jnp.moveaxis(array, 1, 0)
        return moved_axes.reshape((moved_axes.shape[0], blocks, GROUP) + moved_axes.shape[2:])
    outcome = lax.map(head_run, (arrange(delta_query), arrange(delta_key), arrange(delta_value.astype(jnp.float32)), arrange(gate_live), arrange(beta_live)))
    raw_out = jnp.moveaxis(outcome.reshape(H, slot_total, VD), 0, 1)
    raw_out = jnp.where(live_delta[:, None, None], raw_out, 0.0)
    mean_square = lax.optimization_barrier(jnp.mean(raw_out * raw_out, axis=(1, 2)))
    delta_out = (raw_out * lax.rsqrt(mean_square + 1e-06)[:, None, None] * delta_gain).astype(jnp.bfloat16)
    live_attn = slot_in_block < jnp.repeat(attn_count, KEPT_ROW_SLOTS, total_repeat_length=slot_total)
    mark_all = jnp.where(live_attn, attn_position + 1, 0).astype(jnp.int32)
    reach_blocks = max(1, WINDOW // TOK_DEV)
    front_pad = reach_blocks * KEPT_ROW_SLOTS
    padded_key_rows = jnp.concatenate([jnp.zeros((front_pad,) + attn_key.shape[1:], attn_key.dtype), attn_key], axis=0)
    value_pad = jnp.concatenate([jnp.zeros((front_pad,) + attn_value.shape[1:], attn_value.dtype), attn_value], axis=0)
    mark_pad = jnp.concatenate([jnp.zeros((front_pad,), jnp.int32), mark_all], axis=0)

    def one_block(block_index):
        start_row = (block_index * KEPT_ROW_SLOTS).astype(jnp.int32)
        query_rows = lax.dynamic_slice_in_dim(attn_query, start_row, KEPT_ROW_SLOTS, 0)
        query_marks = lax.dynamic_slice_in_dim(mark_all, start_row, KEPT_ROW_SLOTS, 0)
        key_rows = lax.dynamic_slice_in_dim(padded_key_rows, start_row, front_pad + KEPT_ROW_SLOTS, 0)
        value_rows = lax.dynamic_slice_in_dim(value_pad, start_row, front_pad + KEPT_ROW_SLOTS, 0)
        key_marks = lax.dynamic_slice_in_dim(mark_pad, start_row, front_pad + KEPT_ROW_SLOTS, 0)
        return window_attend(query_rows, query_marks, key_rows, value_rows, key_marks)
    attn_out = lax.map(one_block, jnp.arange(N_SEQ, dtype=jnp.int32)).reshape(slot_total, H, VD)
    return (delta_out, attn_out)
```

```python
import jax
import jax.numpy as jnp
from jax import lax
from jax.experimental import pallas as pl
from jax.experimental.pallas import tpu as pltpu
from jax.sharding import Mesh, PartitionSpec as P

ROWS = 256
KD = 128
VD = 256
HEADS = 4
HIDDEN = 8192
WINDOW = 2048
REACH = 4
PART = VD // 4
MARK_ROWS = 16
VMEM_BYTES = 48 * 2**20

SEQ = ("zh", "zl", "x")
f32 = jnp.float32
bf16 = jnp.bfloat16


def halves(x):
    high = x.astype(bf16)
    return high, (x - high.astype(f32)).astype(bf16)


def dot(a, b, dims=((1,), (0,))):
    return lax.dot_general(a, b, (dims, ((), ())), preferred_element_type=f32)


def dot3(a, b):
    ah, al = halves(a)
    bh, bl = halves(b)
    return dot(ah, bh) + (dot(ah, bl) + dot(al, bh))


def dot2(a, b):
    ah, al = halves(a)
    return dot(ah, b) + dot(al, b)


def call(body, out_shape, scalars=0, inputs=1, scratch=()):
    whole = pl.BlockSpec(memory_space=pltpu.VMEM)
    small = pl.BlockSpec(memory_space=pltpu.SMEM)
    return pl.pallas_call(
        body,
        in_specs=[small] * scalars + [whole] * inputs,
        out_specs=jax.tree.map(lambda _: whole, out_shape),
        out_shape=out_shape,
        scratch_shapes=list(scratch),
        compiler_params=pltpu.CompilerParams(vmem_limit_bytes=VMEM_BYTES),
    )


def block_terms(
    count_ref, q_ref, k_ref, v_ref, gate_ref, beta_ref, map_ref, carry_ref, local_ref, x_ref, a_ref
):
    count = count_ref[0]
    row = lax.broadcasted_iota(jnp.int32, (ROWS, ROWS), 0)
    col = lax.broadcasted_iota(jnp.int32, (ROWS, ROWS), 1)
    lane = lax.broadcasted_iota(jnp.int32, (1, ROWS), 1)
    eye = row == col
    kept = []
    for h in range(HEADS):
        k = k_ref[h]
        gate = jnp.where(lane < count, gate_ref[h : h + 1, :], 0.0)
        beta = jnp.where(lane < count, beta_ref[h : h + 1, :], 0.0)
        log_col = jnp.sum(jnp.where(col <= row, gate, 0.0), axis=1, keepdims=True)
        log_row = jnp.sum(jnp.where(eye, log_col, 0.0), axis=0, keepdims=True)
        beta_col = jnp.sum(jnp.where(eye, beta, 0.0), axis=1, keepdims=True)
        gram = dot(k, k, ((1,), (1,)))
        squares = jnp.where(eye, gram, 0.0)
        k_col = lax.rsqrt(jnp.sum(squares, axis=1, keepdims=True) + 1e-6)
        k_row = lax.rsqrt(jnp.sum(squares, axis=0, keepdims=True) + 1e-6)
        decay = jnp.where(col <= row, jnp.exp(jnp.minimum(log_col - log_row, 0.0)), 0.0)
        a = jnp.where(col < row, (beta_col * k_col) * decay * (gram * k_row), 0.0)
        a_ref[h] = a
        x_ref[h] = jnp.where(eye, 1.0, jnp.where((row >> 1) == (col >> 1), -a, 0.0))
        q = q_ref[h]
        wide = q.astype(f32)
        q_col = lax.rsqrt(jnp.sum(wide * wide, axis=1, keepdims=True) + 1e-6)
        local_ref[h] = (q_col * decay) * (dot(q, k, ((1,), (1,))) * k_row)
        kept.append((log_col, log_row, beta, k_col, k_row, q_col))
    step = 1
    while (2 << step) <= ROWS:
        m = 1 << step
        for h in range(HEADS):
            x = x_ref[h]
            if m < 64:
                below = ((row >> (step + 1)) == (col >> (step + 1))) & ((row >> step) != (col >> step))
                x_ref[h] = x - dot3(dot3(x, jnp.where(below, a_ref[h], 0.0)), x)
            else:
                for s in range(0, ROWS, 2 * m):
                    first = x[s : s + m, s : s + m]
                    second = x[s + m : s + 2 * m, s + m : s + 2 * m]
                    between = a_ref[h, s + m : s + 2 * m, s : s + m]
                    x_ref[h, s + m : s + 2 * m, s : s + m] = -dot3(second, dot3(between, first))
        step += 1
    row_k = lax.broadcasted_iota(jnp.int32, (KD, KD), 0)
    col_k = lax.broadcasted_iota(jnp.int32, (KD, KD), 1)
    for h in range(HEADS):
        log_col, log_row, beta, k_col, k_row, q_col = kept[h]
        k = k_ref[h]
        x = x_ref[h]
        new_value = dot2(x * beta, v_ref[h])
        new_key = dot2(x * (beta * jnp.exp(log_row) * k_row), k)
        new = jnp.concatenate([new_key, new_value], axis=1)
        last = log_col[ROWS - 1 : ROWS, :]
        high, low = halves((jnp.exp(last - log_col) * k_col) * new)
        update = dot(k, high, ((0,), (0,))) + dot(k, low, ((0,), (0,)))
        map_ref[h, :, :KD] = jnp.where(row_k == col_k, jnp.exp(last), 0.0) - update[:, :KD]
        map_ref[h, :, KD:] = update[:, KD:]
        mixed = dot3(local_ref[h], new)
        carry_ref[h] = (jnp.exp(log_col) * q_col) * q_ref[h].astype(f32) - mixed[:, :KD]
        local_ref[h] = mixed[:, KD:]


def compose_maps(maps_ref, before_ref, total_ref):
    state = maps_ref[0]
    for i in range(1, 4):
        before_ref[i - 1] = state
        later = maps_ref[i]
        state = dot3(later[:, :KD], state)
        width = state.shape[1]
        state = jnp.concatenate([state[:, :KD], state[:, KD:] + later[:, KD:]], axis=1)
    total_ref[...] = state


def step_state(map_ref, earlier_ref, out_ref):
    out_ref[...] = dot3(map_ref[:, :KD], earlier_ref[:, KD:]) + map_ref[:, KD:]


def group_states(place_ref, earlier_ref, one_ref, two_ref, before_ref, out_ref):
    place = place_ref[0]
    last = dot3(earlier_ref[:, :KD], two_ref[...]) + earlier_ref[:, KD:]
    state = jnp.where(
        place == 0,
        0.0,
        jnp.where(place == 1, earlier_ref[:, KD:], jnp.where(place == 2, one_ref[...], last)),
    )
    out_ref[0] = state
    for i in range(3):
        out_ref[i + 1] = dot3(before_ref[i, :, :KD], state) + before_ref[i, :, KD:]


def plane_states(parts_ref, before_ref, out_ref):
    state = jnp.concatenate([parts_ref[i] for i in range(4)], axis=1)
    out_ref[0] = state
    for i in range(3):
        out_ref[i + 1] = dot3(before_ref[i, :, :KD], state) + before_ref[i, :, KD:]


def raw_rows(carry_ref, local_ref, state_ref, raw_ref, square_ref):
    total = jnp.zeros((ROWS, VD), f32)
    for h in range(HEADS):
        raw = local_ref[h] + dot3(carry_ref[h], state_ref[h])
        raw_ref[h] = raw
        total = total + raw * raw
    column = jnp.sum(total, axis=1, keepdims=True)
    row = lax.broadcasted_iota(jnp.int32, (ROWS, ROWS), 0)
    col = lax.broadcasted_iota(jnp.int32, (ROWS, ROWS), 1)
    square_ref[...] = jnp.broadcast_to(
        jnp.sum(jnp.where(row == col, column, 0.0), axis=0, keepdims=True), square_ref.shape
    )


def attend(q_ref, own_ref, one_ref, two_ref, three_ref, four_ref, out_ref):
    row = lax.broadcasted_iota(jnp.int32, (ROWS, ROWS), 0)
    col = lax.broadcasted_iota(jnp.int32, (ROWS, ROWS), 1)
    blocks = (own_ref, one_ref, two_ref, three_ref, four_ref)

    def marks_of(ref):
        coded = ref[0, ROWS : ROWS + MARK_ROWS, :ROWS].astype(f32)
        return coded[0:1, :] * 256.0 + coded[1:2, :]

    own_marks = marks_of(own_ref)
    query_marks = jnp.sum(jnp.where(row == col, own_marks, 0.0), axis=1, keepdims=True)
    limits = []
    for ref in blocks[:REACH]:
        marks = marks_of(ref)
        limits.append(jnp.where(marks > 0.0, marks, 1e9))
    oldest = marks_of(blocks[REACH])
    oldest = jnp.where(oldest > 0.0, oldest, -1e9)
    for h in range(HEADS):
        q = q_ref[h]
        scores = []
        for d, ref in enumerate(blocks):
            score = dot(q, ref[h, :ROWS, :KD], ((1,), (1,))) * KD**-0.5
            if d < REACH:
                allowed = limits[d] <= query_marks
            else:
                allowed = oldest > query_marks - float(WINDOW)
            scores.append(jnp.where(allowed, score, -1e30))
        top = scores[0]
        for score in scores[1:]:
            top = jnp.maximum(top, score)
        top = jnp.max(top, axis=1, keepdims=True)
        weight_sum = jnp.zeros((ROWS, ROWS), f32)
        mixed = jnp.zeros((ROWS, VD), f32)
        for score, ref in zip(scores, blocks):
            weights = jnp.exp(score - top)
            weight_sum = weight_sum + weights
            mixed = mixed + dot(weights.astype(bf16), ref[h, :ROWS, KD:])
        mixed = mixed / jnp.sum(weight_sum, axis=1, keepdims=True)
        out_ref[h] = jnp.where(query_marks > 0.0, mixed, 0.0).astype(bf16)


def heads_first(block):
    return jnp.swapaxes(block, 0, 1)


def shape_of(*dims, kind=f32):
    return jax.ShapeDtypeStruct(dims, kind)


def window_blocks(key_rows, value_rows, position_rows, count_here):
    marks = jnp.where(jnp.arange(ROWS) < count_here[0], position_rows + 1, 0)
    coded = jnp.stack([marks // 256, marks % 256]).astype(bf16)
    coded = jnp.pad(coded, ((0, MARK_ROWS - 2), (0, KD + VD - ROWS)))
    packed = jnp.concatenate([heads_first(key_rows), heads_first(value_rows)], axis=2)
    coded = jnp.broadcast_to(coded[None], (HEADS,) + coded.shape)
    own = jnp.concatenate([packed, coded], axis=1)
    blocks = [own]
    for distance in range(1, REACH + 1):
        count = lax.axis_size(SEQ)
        route = [(i, i + distance) for i in range(count - distance)]
        blocks.append(lax.ppermute(own, SEQ, route))
    return blocks


def entering_states(maps):
    exchanged = lax.all_to_all(maps, "x", 0, 0, tiled=True)
    plane_before, plane_total = call(
        compose_maps, (shape_of(3, KD, KD + VD), shape_of(KD, KD + VD))
    )(exchanged)
    transition = jnp.broadcast_to(plane_total[None, :, :KD], (4, KD, KD))
    offset = jnp.swapaxes(plane_total[:, KD:].reshape(KD, 4, PART), 0, 1)
    gathered = lax.all_to_all(
        jnp.concatenate([transition, offset], axis=2), "zl", 0, 0, tiled=True
    )
    group_before, group_total = call(
        compose_maps, (shape_of(3, KD, KD + PART), shape_of(KD, KD + PART))
    )(gathered)
    earlier = lax.ppermute(group_total, "zh", [(0, 1), (1, 2), (2, 3)])
    pair = call(step_state, shape_of(KD, PART), inputs=2)(group_total, earlier)
    one = lax.ppermute(pair, "zh", [(1, 2)])
    two = lax.ppermute(pair, "zh", [(1, 3)])
    place = lax.axis_index("zh").astype(jnp.int32).reshape(1)
    planes = call(group_states, shape_of(4, KD, PART), scalars=1, inputs=4)(
        place, earlier, one, two, group_before
    )
    parts = lax.all_to_all(planes, "zl", 0, 0, tiled=True)
    states = call(plane_states, shape_of(4, KD, VD), inputs=2)(parts, plane_before)
    return lax.all_to_all(states, "x", 0, 0, tiled=True)


def shards(
    delta_query,
    delta_key,
    delta_value,
    delta_gate,
    delta_beta,
    delta_count,
    delta_gain,
    attn_query,
    attn_key,
    attn_value,
    attn_position,
    attn_count,
):
    blocks = window_blocks(attn_key, attn_value, attn_position, attn_count)
    maps, carry, local = call(
        block_terms,
        (shape_of(HEADS, KD, KD + VD), shape_of(HEADS, ROWS, KD), shape_of(HEADS, ROWS, VD)),
        scalars=1,
        inputs=5,
        scratch=[pltpu.VMEM((HEADS, ROWS, ROWS), f32)] * 2,
    )(
        delta_count,
        heads_first(delta_query),
        heads_first(delta_key),
        heads_first(delta_value),
        delta_gate.T,
        delta_beta.T,
    )
    states = entering_states(maps)
    attn_heads = call(attend, shape_of(HEADS, ROWS, VD, kind=bf16), inputs=6)(
        heads_first(attn_query), *blocks
    )
    raw, squares = call(
        raw_rows, (shape_of(HEADS, ROWS, VD), shape_of(8, ROWS)), inputs=3
    )(carry, local, states)
    square_sum = jnp.sum(lax.all_gather(squares[0], "head"), axis=0)
    live = jnp.arange(ROWS) < delta_count[0]
    factor = jnp.where(live, lax.rsqrt(square_sum / HIDDEN + 1e-6), 0.0)
    delta_heads = (raw * factor[None, :, None] * delta_gain[:, None, :]).astype(bf16)
    return (heads_first(delta_heads), heads_first(attn_heads))


def solution(mesh):
    grid = Mesh(mesh.devices.reshape(4, 4, 4, 8), SEQ + ("head",))
    rows = P(SEQ, "head", None)
    pairs = P(SEQ, "head")
    block = P(SEQ)
    return jax.shard_map(
        shards,
        mesh=grid,
        in_specs=(rows, rows, rows, pairs, pairs, block, P("head", None), rows, rows, rows, block, block),
        out_specs=(rows, rows),
        check_vma=False,
    )
```

```python
import jax
import jax.numpy as jnp
from jax import lax
from jax.experimental import pallas as pl
from jax.experimental.pallas import tpu as pltpu
from jax.sharding import Mesh, PartitionSpec as P

ROWS = 256
KD = 128
VD = 256
HEADS = 4
HIDDEN = 8192
WINDOW = 2048
PART = VD // 4
MARK_ROWS = 16
VMEM_BYTES = 48 * 2**20

SEQ = ("zh", "zl", "x")
f32 = jnp.float32
bf16 = jnp.bfloat16


def halves(x):
    high = x.astype(bf16)
    return high, (x - high.astype(f32)).astype(bf16)


def dot(a, b, dims=((1,), (0,))):
    return lax.dot_general(a, b, (dims, ((), ())), preferred_element_type=f32)


def dot3(a, b):
    ah, al = halves(a)
    bh, bl = halves(b)
    return dot(ah, bh) + (dot(ah, bl) + dot(al, bh))


def dot2(a, b):
    ah, al = halves(a)
    return dot(ah, b) + dot(al, b)


def call(body, out_shape, scalars=0, inputs=1, scratch=(), flops=1e7):
    whole = pl.BlockSpec(memory_space=pltpu.VMEM)
    small = pl.BlockSpec(memory_space=pltpu.SMEM)
    return pl.pallas_call(
        body,
        in_specs=[small] * scalars + [whole] * inputs,
        out_specs=jax.tree.map(lambda _: whole, out_shape),
        out_shape=out_shape,
        scratch_shapes=list(scratch),
        cost_estimate=pl.CostEstimate(flops=int(flops), bytes_accessed=10**6, transcendentals=0),
        compiler_params=pltpu.CompilerParams(vmem_limit_bytes=VMEM_BYTES),
    )


def block_terms(
    count_ref, q_ref, k_ref, v_ref, gate_ref, beta_ref, map_ref, new_ref, mixing_ref, carry_ref, x_ref, a_ref
):
    count = count_ref[0]
    row = lax.broadcasted_iota(jnp.int32, (ROWS, ROWS), 0)
    col = lax.broadcasted_iota(jnp.int32, (ROWS, ROWS), 1)
    lane = lax.broadcasted_iota(jnp.int32, (1, ROWS), 1)
    eye = row == col
    kept = []
    for h in range(HEADS):
        k = k_ref[h]
        gate = jnp.where(lane < count, gate_ref[h : h + 1, :], 0.0)
        beta = jnp.where(lane < count, beta_ref[h : h + 1, :], 0.0)
        log_col = jnp.sum(jnp.where(col <= row, gate, 0.0), axis=1, keepdims=True)
        log_row = jnp.sum(jnp.where(eye, log_col, 0.0), axis=0, keepdims=True)
        beta_col = jnp.sum(jnp.where(eye, beta, 0.0), axis=1, keepdims=True)
        gram = dot(k, k, ((1,), (1,)))
        squares = jnp.where(eye, gram, 0.0)
        k_col = lax.rsqrt(jnp.sum(squares, axis=1, keepdims=True) + 1e-6)
        k_row = lax.rsqrt(jnp.sum(squares, axis=0, keepdims=True) + 1e-6)
        decay = jnp.where(col <= row, jnp.exp(jnp.minimum(log_col - log_row, 0.0)), 0.0)
        a = jnp.where(col < row, (beta_col * k_col) * decay * (gram * k_row), 0.0)
        a_ref[h] = a
        x_ref[h] = jnp.where(eye, 1.0, jnp.where((row >> 1) == (col >> 1), -a, 0.0))
        q = q_ref[h]
        wide = q.astype(f32)
        q_col = lax.rsqrt(jnp.sum(wide * wide, axis=1, keepdims=True) + 1e-6)
        mixing_ref[h] = (q_col * decay) * (dot(q, k, ((1,), (1,))) * k_row)
        kept.append((log_col, log_row, beta, k_col, k_row, q_col))
    step = 1
    while (2 << step) <= ROWS:
        m = 1 << step
        for h in range(HEADS):
            x = x_ref[h]
            if m < 64:
                below = ((row >> (step + 1)) == (col >> (step + 1))) & ((row >> step) != (col >> step))
                x_ref[h] = x - dot3(dot3(x, jnp.where(below, a_ref[h], 0.0)), x)
            else:
                for s in range(0, ROWS, 2 * m):
                    first = x[s : s + m, s : s + m]
                    second = x[s + m : s + 2 * m, s + m : s + 2 * m]
                    between = a_ref[h, s + m : s + 2 * m, s : s + m]
                    x_ref[h, s + m : s + 2 * m, s : s + m] = -dot3(second, dot3(between, first))
        step += 1
    row_k = lax.broadcasted_iota(jnp.int32, (KD, KD), 0)
    col_k = lax.broadcasted_iota(jnp.int32, (KD, KD), 1)
    for h in range(HEADS):
        log_col, log_row, beta, k_col, k_row, q_col = kept[h]
        k = k_ref[h]
        x = x_ref[h]
        new_value = dot2(x * beta, v_ref[h])
        new_key = dot2(x * (beta * jnp.exp(log_row) * k_row), k)
        new = jnp.concatenate([new_key, new_value], axis=1)
        last = log_col[ROWS - 1 : ROWS, :]
        high, low = halves((jnp.exp(last - log_col) * k_col) * new)
        update = dot(k, high, ((0,), (0,))) + dot(k, low, ((0,), (0,)))
        map_ref[h, :, :KD] = jnp.where(row_k == col_k, jnp.exp(last), 0.0) - update[:, :KD]
        map_ref[h, :, KD:] = update[:, KD:]
        new_ref[h] = new
        carry_ref[h] = (jnp.exp(log_col) * q_col) * q_ref[h].astype(f32)


def row_terms(new_ref, mixing_ref, straight_ref, carry_ref, local_ref):
    for h in range(HEADS):
        mixed = dot3(mixing_ref[h], new_ref[h])
        carry_ref[h] = straight_ref[h] - mixed[:, :KD]
        local_ref[h] = mixed[:, KD:]


def fold(x):
    half = KD // 2
    return jnp.concatenate([x[:half, :], x[half:, :]], axis=1)


def unfold(x):
    return jnp.concatenate([x[:, :PART], x[:, PART:]], axis=0)


def then(state, transition, offset):
    state = dot3(transition, state)
    return jnp.concatenate([state[:, :KD], state[:, KD:] + offset], axis=1)


def compose_plane(maps_ref, before_ref, send_ref):
    state = maps_ref[0]
    for i in range(1, 4):
        before_ref[i - 1] = state
        state = then(state, maps_ref[i, :, :KD], maps_ref[i, :, KD:])
    for i in range(4):
        send_ref[i, :KD, :] = state[:, :KD]
        send_ref[i, KD:, :] = fold(state[:, KD + i * PART : KD + (i + 1) * PART])


def compose_group(maps_ref, before_ref, total_ref, offset_ref):
    state = jnp.concatenate([maps_ref[0, :KD, :], unfold(maps_ref[0, KD:, :])], axis=1)
    for i in range(1, 4):
        before_ref[i - 1] = state
        state = then(state, maps_ref[i, :KD, :], unfold(maps_ref[i, KD:, :]))
    offset = fold(state[:, KD:])
    total_ref[:KD, :] = state[:, :KD]
    total_ref[KD:, :] = offset
    offset_ref[...] = offset


def step_state(map_ref, earlier_ref, out_ref):
    state = dot3(map_ref[:KD, :], unfold(earlier_ref[...]))
    out_ref[...] = fold(state) + map_ref[KD:, :]


def group_states(place_ref, first_ref, one_ref, two_ref, third_ref, before_ref, out_ref):
    place = place_ref[0]
    last = fold(dot3(third_ref[:KD, :], unfold(two_ref[...]))) + third_ref[KD:, :]
    state = jnp.where(
        place == 0,
        0.0,
        jnp.where(place == 1, first_ref[...], jnp.where(place == 2, one_ref[...], last)),
    )
    out_ref[0] = state
    state = unfold(state)
    for i in range(3):
        out_ref[i + 1] = fold(dot3(before_ref[i, :, :KD], state) + before_ref[i, :, KD:])


def plane_states(parts_ref, before_ref, attn_ref, out_ref):
    state = jnp.concatenate([unfold(parts_ref[i]) for i in range(4)], axis=1)
    for i in range(4):
        entering = state
        if i > 0:
            entering = dot3(before_ref[i - 1, :, :KD], state) + before_ref[i - 1, :, KD:]
        out_ref[i, :KD, :], out_ref[i, KD : 2 * KD, :] = halves(entering)
        out_ref[i, 2 * KD :, :] = attn_ref[i]


def raw_rows(carry_ref, local_ref, state_ref, raw_ref, square_ref):
    total = jnp.zeros((ROWS, VD), f32)
    for h in range(HEADS):
        carry_high, carry_low = halves(carry_ref[h])
        high, low = state_ref[h, :KD, :], state_ref[h, KD : 2 * KD, :]
        raw = local_ref[h] + dot(carry_high, high) + (dot(carry_high, low) + dot(carry_low, high))
        raw_ref[h] = raw
        total = total + raw * raw
    column = jnp.sum(total, axis=1, keepdims=True)
    row = lax.broadcasted_iota(jnp.int32, (ROWS, ROWS), 0)
    col = lax.broadcasted_iota(jnp.int32, (ROWS, ROWS), 1)
    square_ref[...] = jnp.broadcast_to(
        jnp.sum(jnp.where(row == col, column, 0.0), axis=0, keepdims=True), square_ref.shape
    )


def normed(count_ref, raw_ref, square_ref, gain_ref, out_ref):
    row = lax.broadcasted_iota(jnp.int32, (ROWS, ROWS), 0)
    col = lax.broadcasted_iota(jnp.int32, (ROWS, ROWS), 1)
    total = square_ref[0:1, :]
    for i in range(1, 8):
        total = total + square_ref[8 * i : 8 * i + 1, :]
    column = jnp.sum(jnp.where(row == col, total, 0.0), axis=1, keepdims=True)
    live = lax.broadcasted_iota(jnp.int32, (ROWS, 1), 0) < count_ref[0]
    factor = jnp.where(live, lax.rsqrt(column * (1.0 / HIDDEN) + 1e-6), 0.0)
    for h in range(HEADS):
        out_ref[h] = (raw_ref[h] * factor * gain_ref[h : h + 1, :]).astype(bf16)


def pack_blocks(count_ref, key_ref, value_ref, query_ref, position_ref, out_ref):
    lane = lax.broadcasted_iota(jnp.int32, (1, ROWS), 1)
    marks = jnp.where(lane < count_ref[0], position_ref[...] + 1, 0)
    spot = lax.broadcasted_iota(jnp.int32, (MARK_ROWS, ROWS), 0)
    coded = jnp.where(spot == 0, marks >> 8, jnp.where(spot == 1, marks & 255, 0))
    coded = coded.astype(f32).astype(bf16)
    for h in range(HEADS):
        out_ref[h, :ROWS, :KD] = key_ref[h]
        out_ref[h, :ROWS, KD : KD + VD] = value_ref[h]
        out_ref[h, :ROWS, KD + VD :] = query_ref[h]
        out_ref[h, ROWS:, :ROWS] = coded
        out_ref[h, ROWS:, ROWS:] = jnp.zeros((MARK_ROWS, 2 * KD + VD - ROWS), bf16)


def attend(here_ref, past_ref, out_ref):
    row = lax.broadcasted_iota(jnp.int32, (ROWS, ROWS), 0)
    col = lax.broadcasted_iota(jnp.int32, (ROWS, ROWS), 1)

    def marks_of(ref, j):
        coded = ref[j, ROWS : ROWS + MARK_ROWS, :ROWS].astype(f32)
        return coded[0:1, :] * 256.0 + coded[1:2, :]

    marks = [marks_of(here_ref, j) for j in range(4)]
    here_marks = [jnp.where(m > 0.0, m, 1e9) for m in marks]
    past_marks = [marks_of(past_ref, j) for j in range(4)]
    past_marks = [jnp.where(m > 0.0, m, 1e9) for m in past_marks]
    for j in range(4):
        query_marks = jnp.sum(jnp.where(row == col, marks[j], 0.0), axis=1, keepdims=True)
        q = here_ref[j, :ROWS, KD + VD :]
        sources = [(here_ref, i, here_marks[i]) for i in range(j + 1)]
        sources += [(past_ref, i, past_marks[i]) for i in range(j, 4)]
        scores = []
        for ref, i, key_marks in sources:
            score = dot(q, ref[i, :ROWS, :KD], ((1,), (1,))) * KD**-0.5
            allowed = (key_marks <= query_marks) & (key_marks > query_marks - float(WINDOW))
            scores.append(jnp.where(allowed, score, -1e30))
        top = scores[0]
        for score in scores[1:]:
            top = jnp.maximum(top, score)
        top = jnp.max(top, axis=1, keepdims=True)
        weight_sum = jnp.zeros((ROWS, ROWS), f32)
        mixed = jnp.zeros((ROWS, VD), f32)
        for score, (ref, i, key_marks) in zip(scores, sources):
            weights = jnp.exp(score - top)
            weight_sum = weight_sum + weights
            mixed = mixed + dot(weights.astype(bf16), ref[i, :ROWS, KD : KD + VD])
        mixed = mixed / jnp.sum(weight_sum, axis=1, keepdims=True)
        out_ref[j] = jnp.where(query_marks > 0.0, mixed, 0.0).astype(bf16)


def heads_first(block):
    return jnp.swapaxes(block, 0, 1)


def shape_of(*dims, kind=f32):
    return jax.ShapeDtypeStruct(dims, kind)


def shards(
    delta_query,
    delta_key,
    delta_value,
    delta_gate,
    delta_beta,
    delta_count,
    delta_gain,
    attn_query,
    attn_key,
    attn_value,
    attn_position,
    attn_count,
):
    packed = call(
        pack_blocks, shape_of(HEADS, ROWS + MARK_ROWS, 2 * KD + VD, kind=bf16), scalars=1, inputs=4
    )(
        attn_count,
        heads_first(attn_key),
        heads_first(attn_value),
        heads_first(attn_query),
        attn_position.reshape(1, ROWS),
    )
    here = lax.all_to_all(packed, "x", 0, 0, tiled=True)
    maps, new, mixing, straight = call(
        block_terms,
        (
            shape_of(HEADS, KD, KD + VD),
            shape_of(HEADS, ROWS, KD + VD),
            shape_of(HEADS, ROWS, ROWS),
            shape_of(HEADS, ROWS, KD),
        ),
        scalars=1,
        inputs=5,
        scratch=[pltpu.VMEM((HEADS, ROWS, ROWS), f32)] * 2,
        flops=8e9,
    )(
        delta_count,
        heads_first(delta_query),
        heads_first(delta_key),
        heads_first(delta_value),
        delta_gate.T,
        delta_beta.T,
    )
    maps, here, past = lax.optimization_barrier((maps, here, here[:, :, : KD + VD]))
    past = lax.ppermute(past, ("zh", "zl"), [(i, i + 1) for i in range(15)])
    exchanged = lax.all_to_all(maps, "x", 0, 0, tiled=True)
    carry, local = call(
        row_terms, (shape_of(HEADS, ROWS, KD), shape_of(HEADS, ROWS, VD)), inputs=3, flops=2e9
    )(new, mixing, straight)
    plane_prefix, plane_total = call(
        compose_plane, (shape_of(3, KD, KD + VD), shape_of(4, KD + PART, KD))
    )(exchanged)
    gathered = lax.all_to_all(plane_total, "zl", 0, 0, tiled=True)
    group_prefix, group_total, group_offset = call(
        compose_group,
        (shape_of(3, KD, KD + PART), shape_of(KD + PART, KD), shape_of(PART, KD)),
    )(gathered)
    first = lax.ppermute(group_offset, "zh", [(0, 1)])
    third = lax.ppermute(group_total, "zh", [(2, 3)])
    pair = call(step_state, shape_of(PART, KD), inputs=2)(group_total, first)
    one = lax.ppermute(pair, "zh", [(1, 2)])
    two = lax.ppermute(pair, "zh", [(1, 3)])
    place = lax.axis_index("zh").astype(jnp.int32).reshape(1)
    planes = call(group_states, shape_of(4, PART, KD), scalars=1, inputs=5)(
        place, first, one, two, third, group_prefix
    )
    planes, past = lax.optimization_barrier((planes, past))
    attn_heads = call(attend, shape_of(4, ROWS, VD, kind=bf16), inputs=2, flops=8e9)(here, past)
    parts = lax.all_to_all(planes, "zl", 0, 0, tiled=True)
    returned = call(plane_states, shape_of(4, 2 * KD + ROWS, VD, kind=bf16), inputs=3)(
        parts, plane_prefix, attn_heads
    )
    states = lax.all_to_all(returned, "x", 0, 0, tiled=True)
    raw, squares = call(
        raw_rows, (shape_of(HEADS, ROWS, VD), shape_of(64, ROWS)), inputs=3
    )(carry, local, states)
    squares = lax.all_to_all(squares, "head", 0, 0, tiled=True)
    delta_heads = call(normed, shape_of(HEADS, ROWS, VD, kind=bf16), scalars=1, inputs=3)(
        delta_count, raw, squares, delta_gain
    )
    return (heads_first(delta_heads), heads_first(states[:, 2 * KD :]))


def solution(mesh):
    grid = Mesh(mesh.devices.reshape(4, 4, 4, 8), SEQ + ("head",))
    rows = P(SEQ, "head", None)
    pairs = P(SEQ, "head")
    block = P(SEQ)
    return jax.shard_map(
        shards,
        mesh=grid,
        in_specs=(rows, rows, rows, pairs, pairs, block, P("head", None), rows, rows, rows, block, block),
        out_specs=(rows, rows),
        check_vma=False,
    )
```

```python
import jax
import jax.numpy as jnp
from jax import lax
from jax.experimental import pallas as pl
from jax.experimental.pallas import tpu as pltpu
from jax.sharding import Mesh, PartitionSpec as P

ROWS = 256
KD = 128
VD = 256
HEADS = 4
HIDDEN = 8192
WINDOW = 2048
PART = VD // 4
MARK_ROWS = 16

SEQ = ("zh", "zl", "x")
f32 = jnp.float32
bf16 = jnp.bfloat16


def halves(x):
    high = x.astype(bf16)
    return high, (x - high.astype(f32)).astype(bf16)


def dot(a, b, dims=((1,), (0,))):
    return lax.dot_general(a, b, (dims, ((), ())), preferred_element_type=f32)


def dot3(a, b):
    ah, al = halves(a)
    bh, bl = halves(b)
    return dot(ah, bh) + (dot(ah, bl) + dot(al, bh))


def dot2(a, b):
    ah, al = halves(a)
    return dot(ah, b) + dot(al, b)


def call(body, out_shape, scalars=0, inputs=1, scratch=(), flops=1e7, mib=8):
    whole = pl.BlockSpec(memory_space=pltpu.VMEM)
    small = pl.BlockSpec(memory_space=pltpu.SMEM)
    return pl.pallas_call(
        body,
        in_specs=[small] * scalars + [whole] * inputs,
        out_specs=jax.tree.map(lambda _: whole, out_shape),
        out_shape=out_shape,
        scratch_shapes=list(scratch),
        cost_estimate=pl.CostEstimate(flops=int(flops), bytes_accessed=10**6, transcendentals=0),
        compiler_params=pltpu.CompilerParams(vmem_limit_bytes=mib * 2**20),
    )


def block_terms(
    count_ref, q_ref, k_ref, v_ref, gate_ref, beta_ref, map_ref, new_ref, mixing_ref, carry_ref, x_ref, a_ref
):
    count = count_ref[0]
    row = lax.broadcasted_iota(jnp.int32, (ROWS, ROWS), 0)
    col = lax.broadcasted_iota(jnp.int32, (ROWS, ROWS), 1)
    lane = lax.broadcasted_iota(jnp.int32, (1, ROWS), 1)
    eye = row == col
    kept = []
    for h in range(HEADS):
        k = k_ref[h]
        gate = jnp.where(lane < count, gate_ref[h : h + 1, :], 0.0)
        beta = jnp.where(lane < count, beta_ref[h : h + 1, :], 0.0)
        log_col = jnp.sum(jnp.where(col <= row, gate, 0.0), axis=1, keepdims=True)
        log_row = jnp.sum(jnp.where(eye, log_col, 0.0), axis=0, keepdims=True)
        beta_col = jnp.sum(jnp.where(eye, beta, 0.0), axis=1, keepdims=True)
        gram = dot(k, k, ((1,), (1,)))
        squares = jnp.where(eye, gram, 0.0)
        k_col = lax.rsqrt(jnp.sum(squares, axis=1, keepdims=True) + 1e-6)
        k_row = lax.rsqrt(jnp.sum(squares, axis=0, keepdims=True) + 1e-6)
        decay = jnp.where(col <= row, jnp.exp(jnp.minimum(log_col - log_row, 0.0)), 0.0)
        a = jnp.where(col < row, (beta_col * k_col) * decay * (gram * k_row), 0.0)
        a_ref[h] = a
        x_ref[h] = jnp.where(eye, 1.0, jnp.where((row >> 1) == (col >> 1), -a, 0.0))
        q = q_ref[h]
        wide = q.astype(f32)
        q_col = lax.rsqrt(jnp.sum(wide * wide, axis=1, keepdims=True) + 1e-6)
        mixing_ref[h] = (q_col * decay) * (dot(q, k, ((1,), (1,))) * k_row)
        kept.append((log_col, log_row, beta, k_col, k_row, q_col))
    step = 1
    while (2 << step) <= ROWS:
        m = 1 << step
        for h in range(HEADS):
            x = x_ref[h]
            if m < 64:
                below = ((row >> (step + 1)) == (col >> (step + 1))) & ((row >> step) != (col >> step))
                x_ref[h] = x - dot3(dot3(x, jnp.where(below, a_ref[h], 0.0)), x)
            else:
                for s in range(0, ROWS, 2 * m):
                    first = x[s : s + m, s : s + m]
                    second = x[s + m : s + 2 * m, s + m : s + 2 * m]
                    between = a_ref[h, s + m : s + 2 * m, s : s + m]
                    x_ref[h, s + m : s + 2 * m, s : s + m] = -dot3(second, dot3(between, first))
        step += 1
    row_k = lax.broadcasted_iota(jnp.int32, (KD, KD), 0)
    col_k = lax.broadcasted_iota(jnp.int32, (KD, KD), 1)
    for h in range(HEADS):
        log_col, log_row, beta, k_col, k_row, q_col = kept[h]
        k = k_ref[h]
        x = x_ref[h]
        new_value = dot2(x * beta, v_ref[h])
        new_key = dot2(x * (beta * jnp.exp(log_row) * k_row), k)
        new = jnp.concatenate([new_key, new_value], axis=1)
        last = log_col[ROWS - 1 : ROWS, :]
        high, low = halves((jnp.exp(last - log_col) * k_col) * new)
        update = dot(k, high, ((0,), (0,))) + dot(k, low, ((0,), (0,)))
        map_ref[h, :, :KD] = jnp.where(row_k == col_k, jnp.exp(last), 0.0) - update[:, :KD]
        map_ref[h, :, KD:] = update[:, KD:]
        new_ref[h] = new
        carry_ref[h] = (jnp.exp(log_col) * q_col) * q_ref[h].astype(f32)


def row_terms(new_ref, mixing_ref, straight_ref, carry_ref, local_ref):
    for h in range(HEADS):
        mixed = dot3(mixing_ref[h], new_ref[h])
        carry_ref[h] = straight_ref[h] - mixed[:, :KD]
        local_ref[h] = mixed[:, KD:]


def fold(x):
    half = KD // 2
    return jnp.concatenate([x[:half, :], x[half:, :]], axis=1)


def unfold(x):
    return jnp.concatenate([x[:, :PART], x[:, PART:]], axis=0)


def then(state, transition, offset):
    state = dot3(transition, state)
    return jnp.concatenate([state[:, :KD], state[:, KD:] + offset], axis=1)


def compose_plane(maps_ref, before_ref, send_ref):
    state = maps_ref[0]
    for i in range(1, 4):
        before_ref[i - 1] = state
        state = then(state, maps_ref[i, :, :KD], maps_ref[i, :, KD:])
    for i in range(4):
        send_ref[i, :KD, :] = state[:, :KD]
        send_ref[i, KD:, :] = fold(state[:, KD + i * PART : KD + (i + 1) * PART])


def compose_group(maps_ref, before_ref, total_ref, offset_ref):
    state = jnp.concatenate([maps_ref[0, :KD, :], unfold(maps_ref[0, KD:, :])], axis=1)
    for i in range(1, 4):
        before_ref[i - 1] = state
        state = then(state, maps_ref[i, :KD, :], unfold(maps_ref[i, KD:, :]))
    offset = fold(state[:, KD:])
    total_ref[:KD, :] = state[:, :KD]
    total_ref[KD:, :] = offset
    offset_ref[...] = offset


def step_state(map_ref, earlier_ref, out_ref):
    state = dot3(map_ref[:KD, :], unfold(earlier_ref[...]))
    out_ref[...] = fold(state) + map_ref[KD:, :]


def group_states(place_ref, first_ref, one_ref, two_ref, third_ref, before_ref, out_ref):
    place = place_ref[0]
    last = fold(dot3(third_ref[:KD, :], unfold(two_ref[...]))) + third_ref[KD:, :]
    state = jnp.where(
        place == 0,
        0.0,
        jnp.where(place == 1, first_ref[...], jnp.where(place == 2, one_ref[...], last)),
    )
    out_ref[0] = state
    state = unfold(state)
    for i in range(3):
        out_ref[i + 1] = fold(dot3(before_ref[i, :, :KD], state) + before_ref[i, :, KD:])


def plane_states(parts_ref, before_ref, attn_ref, out_ref):
    state = jnp.concatenate([unfold(parts_ref[i]) for i in range(4)], axis=1)
    for i in range(4):
        entering = state
        if i > 0:
            entering = dot3(before_ref[i - 1, :, :KD], state) + before_ref[i - 1, :, KD:]
        out_ref[i, :KD, :], out_ref[i, KD : 2 * KD, :] = halves(entering)
        out_ref[i, 2 * KD :, :] = attn_ref[i]


def raw_rows(carry_ref, local_ref, state_ref, raw_ref, square_ref):
    total = jnp.zeros((ROWS, VD), f32)
    for h in range(HEADS):
        carry_high, carry_low = halves(carry_ref[h])
        high, low = state_ref[h, :KD, :], state_ref[h, KD : 2 * KD, :]
        raw = local_ref[h] + dot(carry_high, high) + (dot(carry_high, low) + dot(carry_low, high))
        raw_ref[h] = raw
        total = total + raw * raw
    column = jnp.sum(total, axis=1, keepdims=True)
    row = lax.broadcasted_iota(jnp.int32, (ROWS, ROWS), 0)
    col = lax.broadcasted_iota(jnp.int32, (ROWS, ROWS), 1)
    square_ref[...] = jnp.broadcast_to(
        jnp.sum(jnp.where(row == col, column, 0.0), axis=0, keepdims=True), square_ref.shape
    )


def normed(count_ref, raw_ref, square_ref, gain_ref, out_ref):
    row = lax.broadcasted_iota(jnp.int32, (ROWS, ROWS), 0)
    col = lax.broadcasted_iota(jnp.int32, (ROWS, ROWS), 1)
    total = square_ref[0:1, :]
    for i in range(1, 8):
        total = total + square_ref[8 * i : 8 * i + 1, :]
    column = jnp.sum(jnp.where(row == col, total, 0.0), axis=1, keepdims=True)
    live = lax.broadcasted_iota(jnp.int32, (ROWS, 1), 0) < count_ref[0]
    factor = jnp.where(live, lax.rsqrt(column * (1.0 / HIDDEN) + 1e-6), 0.0)
    for h in range(HEADS):
        out_ref[h] = (raw_ref[h] * factor * gain_ref[h : h + 1, :]).astype(bf16)


def pack_keys(count_ref, key_ref, value_ref, position_ref, out_ref):
    lane = lax.broadcasted_iota(jnp.int32, (1, ROWS), 1)
    marks = jnp.where(lane < count_ref[0], position_ref[...] + 1, 0)
    spot = lax.broadcasted_iota(jnp.int32, (MARK_ROWS, ROWS), 0)
    coded = jnp.where(spot == 0, marks >> 8, jnp.where(spot == 1, marks & 255, 0))
    coded = coded.astype(f32).astype(bf16)
    for h in range(HEADS):
        out_ref[h, :ROWS, :KD] = key_ref[h]
        out_ref[h, :ROWS, KD:] = value_ref[h]
        out_ref[h, ROWS:, :ROWS] = coded
        out_ref[h, ROWS:, ROWS:] = jnp.zeros((MARK_ROWS, KD + VD - ROWS), bf16)


def pack_heads(place_ref, query_ref, keys_ref, past_ref, *out_refs):
    for d, out_ref in enumerate(out_refs):
        h = lax.rem(place_ref[0] + d, 4)
        out_ref[:, : KD + VD] = keys_ref[pl.ds(h, 1)][0]
        out_ref[:ROWS, KD + VD : 2 * KD + VD] = query_ref[pl.ds(h, 1)][0]
        out_ref[ROWS:, KD + VD : 2 * KD + VD] = jnp.zeros((MARK_ROWS, KD), bf16)
        out_ref[:, 2 * KD + VD :] = past_ref[pl.ds(h, 1)][0]


def attend(place_ref, own_ref, one_ref, two_ref, three_ref, out_ref):
    here = place_ref[0]
    row = lax.broadcasted_iota(jnp.int32, (ROWS, ROWS), 0)
    col = lax.broadcasted_iota(jnp.int32, (ROWS, ROWS), 1)
    blocks = (own_ref, one_ref, two_ref, three_ref)
    before = 2 * KD + VD

    def marks_of(ref, start):
        coded = ref[ROWS : ROWS + MARK_ROWS, start : start + ROWS].astype(f32)
        marks = coded[0:1, :] * 256.0 + coded[1:2, :]
        return marks, jnp.where(marks > 0.0, marks, 1e9)

    marks = [marks_of(ref, 0) for ref in blocks]
    past_marks = [marks_of(ref, before) for ref in blocks]
    spots = [lax.rem(here - j + 4, 4) for j in range(4)]
    for j in range(4):
        query_marks = jnp.sum(jnp.where(row == col, marks[j][0], 0.0), axis=1, keepdims=True)
        q = blocks[j][:ROWS, KD + VD : before]
        both = (blocks[j][:ROWS, : KD + VD], blocks[j][:ROWS, before:])
        sources = [(both[0], marks[j][1]), (both[1], past_marks[j][1])]
        for i in range(4):
            if i != j:
                same = spots[i] < spots[j]
                keys = jnp.where(same, blocks[i][:ROWS, : KD + VD], blocks[i][:ROWS, before:])
                sources.append((keys, jnp.where(same, marks[i][1], past_marks[i][1])))
        scores = []
        for keys, key_marks in sources:
            score = dot(q, keys[:, :KD], ((1,), (1,))) * KD**-0.5
            allowed = (key_marks <= query_marks) & (key_marks > query_marks - float(WINDOW))
            scores.append(jnp.where(allowed, score, -1e30))
        top = scores[0]
        for score in scores[1:]:
            top = jnp.maximum(top, score)
        top = jnp.max(top, axis=1, keepdims=True)
        weight_sum = jnp.zeros((ROWS, ROWS), f32)
        mixed = jnp.zeros((ROWS, VD), f32)
        for score, (keys, key_marks) in zip(scores, sources):
            weights = jnp.exp(score - top)
            weight_sum = weight_sum + weights
            mixed = mixed + dot(weights.astype(bf16), keys[:, KD:])
        mixed = mixed / jnp.sum(weight_sum, axis=1, keepdims=True)
        out_ref[pl.ds(spots[j], 1)] = jnp.where(query_marks > 0.0, mixed, 0.0).astype(bf16)[None]


def heads_first(block):
    return jnp.swapaxes(block, 0, 1)


def shape_of(*dims, kind=f32):
    return jax.ShapeDtypeStruct(dims, kind)


def shards(
    delta_query,
    delta_key,
    delta_value,
    delta_gate,
    delta_beta,
    delta_count,
    delta_gain,
    attn_query,
    attn_key,
    attn_value,
    attn_position,
    attn_count,
):
    maps, new, mixing, straight = call(
        block_terms,
        (
            shape_of(HEADS, KD, KD + VD),
            shape_of(HEADS, ROWS, KD + VD),
            shape_of(HEADS, ROWS, ROWS),
            shape_of(HEADS, ROWS, KD),
        ),
        scalars=1,
        inputs=5,
        scratch=[pltpu.VMEM((HEADS, ROWS, ROWS), f32)] * 2,
        flops=8e9,
        mib=16,
    )(
        delta_count,
        heads_first(delta_query),
        heads_first(delta_key),
        heads_first(delta_value),
        delta_gate.T,
        delta_beta.T,
    )
    maps, attn_key, attn_value, attn_query = lax.optimization_barrier(
        (maps, attn_key, attn_value, attn_query)
    )
    exchanged = lax.all_to_all(maps, "x", 0, 0, tiled=True)
    keys = call(
        pack_keys, shape_of(HEADS, ROWS + MARK_ROWS, KD + VD, kind=bf16), scalars=1, inputs=3
    )(attn_count, heads_first(attn_key), heads_first(attn_value), attn_position.reshape(1, ROWS))
    past = lax.ppermute(keys, ("zh", "zl"), [(i, i + 1) for i in range(15)])
    spot = lax.axis_index("x").astype(jnp.int32).reshape(1)
    carry, local = call(
        row_terms, (shape_of(HEADS, ROWS, KD), shape_of(HEADS, ROWS, VD)), inputs=3, flops=2e9
    )(new, mixing, straight)
    plane_prefix, plane_total = call(
        compose_plane, (shape_of(3, KD, KD + VD), shape_of(4, KD + PART, KD))
    )(exchanged)
    _, past = lax.optimization_barrier((plane_total, past))
    width = 3 * KD + 2 * VD
    blocks = call(
        pack_heads, (shape_of(ROWS + MARK_ROWS, width, kind=bf16),) * 4, scalars=1, inputs=3
    )(spot, heads_first(attn_query), keys, past)
    blocks = [
        lax.ppermute(block, "x", [(i, (i + d) % 4) for i in range(4)]) if d else block
        for d, block in enumerate(blocks)
    ]
    gathered = lax.all_to_all(plane_total, "zl", 0, 0, tiled=True)
    group_prefix, group_total, group_offset = call(
        compose_group,
        (shape_of(3, KD, KD + PART), shape_of(KD + PART, KD), shape_of(PART, KD)),
    )(gathered)
    first = lax.ppermute(group_offset, "zh", [(0, 1)])
    third = lax.ppermute(group_total, "zh", [(2, 3)])
    pair = call(step_state, shape_of(PART, KD), inputs=2)(group_total, first)
    pair, third = lax.optimization_barrier((pair, third))
    one = lax.ppermute(pair, "zh", [(1, 2)])
    two = lax.ppermute(pair, "zh", [(1, 3)])
    place = lax.axis_index("zh").astype(jnp.int32).reshape(1)
    planes = call(group_states, shape_of(4, PART, KD), scalars=1, inputs=5)(
        place, first, one, two, third, group_prefix
    )
    planes, *blocks = lax.optimization_barrier((planes, *blocks))
    attn_heads = call(
        attend, shape_of(4, ROWS, VD, kind=bf16), scalars=1, inputs=4, flops=8e9, mib=16
    )(spot, *blocks)
    parts = lax.all_to_all(planes, "zl", 0, 0, tiled=True)
    returned = call(plane_states, shape_of(4, 2 * KD + ROWS, VD, kind=bf16), inputs=3)(
        parts, plane_prefix, attn_heads
    )
    states = lax.all_to_all(returned, "x", 0, 0, tiled=True)
    raw, squares = call(
        raw_rows, (shape_of(HEADS, ROWS, VD), shape_of(64, ROWS)), inputs=3
    )(carry, local, states)
    squares = lax.all_to_all(squares, "head", 0, 0, tiled=True)
    delta_heads = call(normed, shape_of(HEADS, ROWS, VD, kind=bf16), scalars=1, inputs=3)(
        delta_count, raw, squares, delta_gain
    )
    return (heads_first(delta_heads), heads_first(states[:, 2 * KD :]))


def solution(mesh):
    grid = Mesh(mesh.devices.reshape(4, 4, 4, 8), SEQ + ("head",))
    rows = P(SEQ, "head", None)
    pairs = P(SEQ, "head")
    block = P(SEQ)
    return jax.shard_map(
        shards,
        mesh=grid,
        in_specs=(rows, rows, rows, pairs, pairs, block, P("head", None), rows, rows, rows, block, block),
        out_specs=(rows, rows),
        check_vma=False,
    )
```

```python
import jax
import jax.numpy as jnp
from jax import lax
from jax.experimental import pallas as pl
from jax.experimental.pallas import tpu as pltpu
from jax.sharding import Mesh, PartitionSpec as P

ROWS = 256
KD = 128
VD = 256
HEADS = 4
HIDDEN = 8192
WINDOW = 2048
PART = VD // 4
MARK_ROWS = 16

SEQ = ("zh", "zl", "x")
f32 = jnp.float32
bf16 = jnp.bfloat16


def halves(x):
    high = x.astype(bf16)
    return high, (x - high.astype(f32)).astype(bf16)


def dot(a, b, dims=((1,), (0,))):
    return lax.dot_general(a, b, (dims, ((), ())), preferred_element_type=f32)


def dot3(a, b):
    ah, al = halves(a)
    bh, bl = halves(b)
    return dot(ah, bh) + (dot(ah, bl) + dot(al, bh))


def dot2(a, b):
    ah, al = halves(a)
    return dot(ah, b) + dot(al, b)


def call(body, out_shape, scalars=0, inputs=1, scratch=(), flops=1e7, mib=8):
    whole = pl.BlockSpec(memory_space=pltpu.VMEM)
    small = pl.BlockSpec(memory_space=pltpu.SMEM)
    return pl.pallas_call(
        body,
        in_specs=[small] * scalars + [whole] * inputs,
        out_specs=jax.tree.map(lambda _: whole, out_shape),
        out_shape=out_shape,
        scratch_shapes=list(scratch),
        cost_estimate=pl.CostEstimate(flops=int(flops), bytes_accessed=10**6, transcendentals=0),
        compiler_params=pltpu.CompilerParams(vmem_limit_bytes=mib * 2**20),
    )


def block_terms(
    count_ref, q_ref, k_ref, v_ref, gate_ref, beta_ref, map_ref, carry_ref, local_ref, x_ref, a_ref
):
    count = count_ref[0]
    row = lax.broadcasted_iota(jnp.int32, (ROWS, ROWS), 0)
    col = lax.broadcasted_iota(jnp.int32, (ROWS, ROWS), 1)
    lane = lax.broadcasted_iota(jnp.int32, (1, ROWS), 1)
    eye = row == col
    kept = []
    for h in range(HEADS):
        k = k_ref[h]
        gate = jnp.where(lane < count, gate_ref[h : h + 1, :], 0.0)
        beta = jnp.where(lane < count, beta_ref[h : h + 1, :], 0.0)
        log_col = jnp.sum(jnp.where(col <= row, gate, 0.0), axis=1, keepdims=True)
        log_row = jnp.sum(jnp.where(eye, log_col, 0.0), axis=0, keepdims=True)
        beta_col = jnp.sum(jnp.where(eye, beta, 0.0), axis=1, keepdims=True)
        gram = dot(k, k, ((1,), (1,)))
        squares = jnp.where(eye, gram, 0.0)
        k_col = lax.rsqrt(jnp.sum(squares, axis=1, keepdims=True) + 1e-6)
        k_row = lax.rsqrt(jnp.sum(squares, axis=0, keepdims=True) + 1e-6)
        decay = jnp.where(col <= row, jnp.exp(jnp.minimum(log_col - log_row, 0.0)), 0.0)
        a = jnp.where(col < row, (beta_col * k_col) * decay * (gram * k_row), 0.0)
        a_ref[h] = a
        x_ref[h] = jnp.where(eye, 1.0, jnp.where((row >> 1) == (col >> 1), -a, 0.0))
        q = q_ref[h]
        wide = q.astype(f32)
        q_col = lax.rsqrt(jnp.sum(wide * wide, axis=1, keepdims=True) + 1e-6)
        local_ref[h] = (q_col * decay) * (dot(q, k, ((1,), (1,))) * k_row)
        kept.append((log_col, log_row, beta, k_col, k_row, q_col))
    step = 1
    while (2 << step) <= ROWS:
        m = 1 << step
        for h in range(HEADS):
            x = x_ref[h]
            if m < 64:
                below = ((row >> (step + 1)) == (col >> (step + 1))) & ((row >> step) != (col >> step))
                x_ref[h] = x - dot3(dot3(x, jnp.where(below, a_ref[h], 0.0)), x)
            else:
                for s in range(0, ROWS, 2 * m):
                    first = x[s : s + m, s : s + m]
                    second = x[s + m : s + 2 * m, s + m : s + 2 * m]
                    between = a_ref[h, s + m : s + 2 * m, s : s + m]
                    x_ref[h, s + m : s + 2 * m, s : s + m] = -dot3(second, dot3(between, first))
        step += 1
    row_k = lax.broadcasted_iota(jnp.int32, (KD, KD), 0)
    col_k = lax.broadcasted_iota(jnp.int32, (KD, KD), 1)
    for h in range(HEADS):
        log_col, log_row, beta, k_col, k_row, q_col = kept[h]
        k = k_ref[h]
        x = x_ref[h]
        new_value = dot2(x * beta, v_ref[h])
        new_key = dot2(x * (beta * jnp.exp(log_row) * k_row), k)
        new = jnp.concatenate([new_key, new_value], axis=1)
        last = log_col[ROWS - 1 : ROWS, :]
        high, low = halves((jnp.exp(last - log_col) * k_col) * new)
        update = dot(k, high, ((0,), (0,))) + dot(k, low, ((0,), (0,)))
        map_ref[h, :, :KD] = jnp.where(row_k == col_k, jnp.exp(last), 0.0) - update[:, :KD]
        map_ref[h, :, KD:] = update[:, KD:]
        mixed = dot3(local_ref[h], new)
        carry_ref[h] = (jnp.exp(log_col) * q_col) * q_ref[h].astype(f32) - mixed[:, :KD]
        local_ref[h] = mixed[:, KD:]


def fold(x):
    half = KD // 2
    return jnp.concatenate([x[:half, :], x[half:, :]], axis=1)


def unfold(x):
    return jnp.concatenate([x[:, :PART], x[:, PART:]], axis=0)


def then(state, transition, offset):
    state = dot3(transition, state)
    return jnp.concatenate([state[:, :KD], state[:, KD:] + offset], axis=1)


def pick(index, choices):
    picked = choices[0]
    for i in range(1, len(choices)):
        picked = jnp.where(index == i, choices[i], picked)
    return picked


def ahead(place, shift):
    return lax.rem(place + shift, 4)


def compose_plane(place_ref, maps_ref, before_ref, *send_refs):
    state = maps_ref[0]
    for i in range(1, 4):
        before_ref[i - 1] = state
        state = then(state, maps_ref[i, :, :KD], maps_ref[i, :, KD:])
    quarters = [fold(state[:, KD + i * PART : KD + (i + 1) * PART]) for i in range(4)]
    for d, send_ref in enumerate(send_refs):
        send_ref[:KD, :] = state[:, :KD]
        send_ref[KD:, :] = pick(ahead(place_ref[0], d), quarters)


def in_order(place, refs, ordered_ref):
    for d, ref in enumerate(refs):
        ordered_ref[pl.ds(ahead(place, 4 - d), 1)] = ref[...][None]


def compose_group(
    place_ref, own_ref, one_ref, two_ref, three_ref, before_ref, total_ref, offset_ref, maps_ref
):
    in_order(place_ref[0], (own_ref, one_ref, two_ref, three_ref), maps_ref)
    state = jnp.concatenate([maps_ref[0, :KD, :], unfold(maps_ref[0, KD:, :])], axis=1)
    for i in range(1, 4):
        before_ref[i - 1] = state
        state = then(state, maps_ref[i, :KD, :], unfold(maps_ref[i, KD:, :]))
    offset = fold(state[:, KD:])
    total_ref[:KD, :] = state[:, :KD]
    total_ref[KD:, :] = offset
    offset_ref[...] = offset


def step_state(map_ref, earlier_ref, out_ref):
    state = dot3(map_ref[:KD, :], unfold(earlier_ref[...]))
    out_ref[...] = fold(state) + map_ref[KD:, :]


def group_states(place_ref, first_ref, one_ref, two_ref, third_ref, before_ref, *out_refs):
    group = place_ref[0]
    last = fold(dot3(third_ref[:KD, :], unfold(two_ref[...]))) + third_ref[KD:, :]
    entering = pick(group, [jnp.zeros_like(last), first_ref[...], one_ref[...], last])
    state = unfold(entering)
    planes = [entering]
    for i in range(3):
        planes.append(fold(dot3(before_ref[i, :, :KD], state) + before_ref[i, :, KD:]))
    for d, out_ref in enumerate(out_refs):
        out_ref[...] = pick(ahead(place_ref[1], d), planes)


def plane_states(
    place_ref, own_ref, one_ref, two_ref, three_ref, before_ref, out_ref, parts_ref
):
    in_order(place_ref[0], (own_ref, one_ref, two_ref, three_ref), parts_ref)
    state = jnp.concatenate([unfold(parts_ref[i]) for i in range(4)], axis=1)
    out_ref[0] = state
    for i in range(3):
        out_ref[i + 1] = dot3(before_ref[i, :, :KD], state) + before_ref[i, :, KD:]


def raw_rows(carry_ref, local_ref, state_ref, raw_ref, square_ref):
    total = jnp.zeros((ROWS, VD), f32)
    for h in range(HEADS):
        raw = local_ref[h] + dot3(carry_ref[h], state_ref[h])
        raw_ref[h] = raw
        total = total + raw * raw
    column = jnp.sum(total, axis=1, keepdims=True)
    row = lax.broadcasted_iota(jnp.int32, (ROWS, ROWS), 0)
    col = lax.broadcasted_iota(jnp.int32, (ROWS, ROWS), 1)
    square_ref[...] = jnp.broadcast_to(
        jnp.sum(jnp.where(row == col, column, 0.0), axis=0, keepdims=True), square_ref.shape
    )


def normed(count_ref, raw_ref, square_ref, gain_ref, out_ref):
    row = lax.broadcasted_iota(jnp.int32, (ROWS, ROWS), 0)
    col = lax.broadcasted_iota(jnp.int32, (ROWS, ROWS), 1)
    total = square_ref[0:1, :]
    for i in range(1, 8):
        total = total + square_ref[8 * i : 8 * i + 1, :]
    column = jnp.sum(jnp.where(row == col, total, 0.0), axis=1, keepdims=True)
    live = lax.broadcasted_iota(jnp.int32, (ROWS, 1), 0) < count_ref[0]
    factor = jnp.where(live, lax.rsqrt(column * (1.0 / HIDDEN) + 1e-6), 0.0)
    for h in range(HEADS):
        out_ref[h] = (raw_ref[h] * factor * gain_ref[h : h + 1, :]).astype(bf16)


def pack_blocks(count_ref, key_ref, value_ref, query_ref, position_ref, out_ref):
    lane = lax.broadcasted_iota(jnp.int32, (1, ROWS), 1)
    marks = jnp.where(lane < count_ref[0], position_ref[...] + 1, 0)
    spot = lax.broadcasted_iota(jnp.int32, (MARK_ROWS, ROWS), 0)
    coded = jnp.where(spot == 0, marks >> 8, jnp.where(spot == 1, marks & 255, 0))
    coded = coded.astype(f32).astype(bf16)
    for h in range(HEADS):
        out_ref[h, :ROWS, :KD] = key_ref[h]
        out_ref[h, :ROWS, KD : KD + VD] = value_ref[h]
        out_ref[h, :ROWS, KD + VD :] = query_ref[h]
        out_ref[h, ROWS:, :ROWS] = coded
        out_ref[h, ROWS:, ROWS:] = jnp.zeros((MARK_ROWS, 2 * KD + VD - ROWS), bf16)


def attend(place_ref, here_ref, past_ref, *refs):
    out_refs, rows_ref = refs[:4], refs[4]
    row = lax.broadcasted_iota(jnp.int32, (ROWS, ROWS), 0)
    col = lax.broadcasted_iota(jnp.int32, (ROWS, ROWS), 1)

    def marks_of(ref, j):
        coded = ref[j, ROWS : ROWS + MARK_ROWS, :ROWS].astype(f32)
        return coded[0:1, :] * 256.0 + coded[1:2, :]

    marks = [marks_of(here_ref, j) for j in range(4)]
    here_marks = [jnp.where(m > 0.0, m, 1e9) for m in marks]
    past_marks = [marks_of(past_ref, j) for j in range(4)]
    past_marks = [jnp.where(m > 0.0, m, 1e9) for m in past_marks]
    for j in range(4):
        query_marks = jnp.sum(jnp.where(row == col, marks[j], 0.0), axis=1, keepdims=True)
        q = here_ref[j, :ROWS, KD + VD :]
        sources = [(here_ref, i, here_marks[i]) for i in range(j + 1)]
        sources += [(past_ref, i, past_marks[i]) for i in range(j, 4)]
        scores = []
        for ref, i, key_marks in sources:
            score = dot(q, ref[i, :ROWS, :KD], ((1,), (1,))) * KD**-0.5
            allowed = (key_marks <= query_marks) & (key_marks > query_marks - float(WINDOW))
            scores.append(jnp.where(allowed, score, -1e30))
        top = scores[0]
        for score in scores[1:]:
            top = jnp.maximum(top, score)
        top = jnp.max(top, axis=1, keepdims=True)
        weight_sum = jnp.zeros((ROWS, ROWS), f32)
        mixed = jnp.zeros((ROWS, VD), f32)
        for score, (ref, i, key_marks) in zip(scores, sources):
            weights = jnp.exp(score - top)
            weight_sum = weight_sum + weights
            mixed = mixed + dot(weights.astype(bf16), ref[i, :ROWS, KD : KD + VD])
        mixed = mixed / jnp.sum(weight_sum, axis=1, keepdims=True)
        rows_ref[j] = jnp.where(query_marks > 0.0, mixed, 0.0).astype(bf16)
    for d, out_ref in enumerate(out_refs):
        out_ref[...] = rows_ref[pl.ds(ahead(place_ref[0], d), 1)][0]


def gather_heads(place_ref, own_ref, one_ref, two_ref, three_ref, out_ref):
    in_order(place_ref[0], (own_ref, one_ref, two_ref, three_ref), out_ref)


def heads_first(block):
    return jnp.swapaxes(block, 0, 1)


def around(parts, axis):
    return [
        lax.ppermute(part, axis, [(i, (i + d) % 4) for i in range(4)]) if d else part
        for d, part in enumerate(parts)
    ]


def shape_of(*dims, kind=f32):
    return jax.ShapeDtypeStruct(dims, kind)


def shards(
    delta_query,
    delta_key,
    delta_value,
    delta_gate,
    delta_beta,
    delta_count,
    delta_gain,
    attn_query,
    attn_key,
    attn_value,
    attn_position,
    attn_count,
):
    zh, zl, x = (lax.axis_index(name).astype(jnp.int32).reshape(1) for name in SEQ)
    maps, carry, local = call(
        block_terms,
        (shape_of(HEADS, KD, KD + VD), shape_of(HEADS, ROWS, KD), shape_of(HEADS, ROWS, VD)),
        scalars=1,
        inputs=5,
        scratch=[pltpu.VMEM((HEADS, ROWS, ROWS), f32)] * 2,
        flops=8e9,
        mib=16,
    )(
        delta_count,
        heads_first(delta_query),
        heads_first(delta_key),
        heads_first(delta_value),
        delta_gate.T,
        delta_beta.T,
    )
    maps, attn_key, attn_value, attn_query = lax.optimization_barrier(
        (maps, attn_key, attn_value, attn_query)
    )
    exchanged = lax.all_to_all(maps, "x", 0, 0, tiled=True)
    packed = call(
        pack_blocks, shape_of(HEADS, ROWS + MARK_ROWS, 2 * KD + VD, kind=bf16), scalars=1, inputs=4
    )(
        attn_count,
        heads_first(attn_key),
        heads_first(attn_value),
        heads_first(attn_query),
        attn_position.reshape(1, ROWS),
    )
    plane_prefix, *plane_totals = call(
        compose_plane,
        (shape_of(3, KD, KD + VD),) + (shape_of(KD + PART, KD),) * 4,
        scalars=1,
    )(zl, exchanged)
    _, packed = lax.optimization_barrier((plane_totals[0], packed))
    plane_totals = around(plane_totals, "zl")
    here = lax.all_to_all(packed, "x", 0, 0, tiled=True)
    group_prefix, group_total, group_offset = call(
        compose_group,
        (shape_of(3, KD, KD + PART), shape_of(KD + PART, KD), shape_of(PART, KD)),
        scalars=1,
        inputs=4,
        scratch=[pltpu.VMEM((4, KD + PART, KD), f32)],
    )(zl, *plane_totals)
    first = lax.ppermute(group_offset, "zh", [(0, 1)])
    third = lax.ppermute(group_total, "zh", [(2, 3)])
    _, here = lax.optimization_barrier((first, here))
    past = lax.ppermute(here[:, :, : KD + VD], ("zh", "zl"), [(i, i + 1) for i in range(15)])
    pair = call(step_state, shape_of(PART, KD), inputs=2)(group_total, first)
    one = lax.ppermute(pair, "zh", [(1, 2)])
    two = lax.ppermute(pair, "zh", [(1, 3)])
    planes = call(group_states, (shape_of(PART, KD),) * 4, scalars=1, inputs=5)(
        jnp.concatenate([zh, zl]), first, one, two, third, group_prefix
    )
    states = call(
        plane_states,
        shape_of(4, KD, VD),
        scalars=1,
        inputs=5,
        scratch=[pltpu.VMEM((4, PART, KD), f32)],
    )(zl, *around(planes, "zl"), plane_prefix)
    _, here, past = lax.optimization_barrier((states, here, past))
    attn_rows = call(
        attend,
        (shape_of(ROWS, VD, kind=bf16),) * 4,
        scalars=1,
        inputs=2,
        scratch=[pltpu.VMEM((4, ROWS, VD), bf16)],
        flops=8e9,
        mib=16,
    )(x, here, past)
    attn_rows = around(attn_rows, "x")
    states = lax.all_to_all(states, "x", 0, 0, tiled=True)
    raw, squares = call(
        raw_rows, (shape_of(HEADS, ROWS, VD), shape_of(64, ROWS)), inputs=3
    )(carry, local, states)
    squares = lax.all_to_all(squares, "head", 0, 0, tiled=True)
    attn_heads = call(
        gather_heads, shape_of(HEADS, ROWS, VD, kind=bf16), scalars=1, inputs=4
    )(x, *attn_rows)
    squares, attn_heads = lax.optimization_barrier((squares, attn_heads))
    delta_heads = call(normed, shape_of(HEADS, ROWS, VD, kind=bf16), scalars=1, inputs=3)(
        delta_count, raw, squares, delta_gain
    )
    return (heads_first(delta_heads), heads_first(attn_heads))


def solution(mesh):
    grid = Mesh(mesh.devices.reshape(4, 4, 4, 8), SEQ + ("head",))
    rows = P(SEQ, "head", None)
    pairs = P(SEQ, "head")
    block = P(SEQ)
    return jax.shard_map(
        shards,
        mesh=grid,
        in_specs=(rows, rows, rows, pairs, pairs, block, P("head", None), rows, rows, rows, block, block),
        out_specs=(rows, rows),
        check_vma=False,
    )
```

```python
import jax
import jax.numpy as jnp
from jax import lax
from jax.experimental import pallas as pl
from jax.experimental.pallas import tpu as pltpu
from jax.sharding import Mesh, PartitionSpec as P

ROWS = 256
KD = 128
VD = 256
HEADS = 4
HIDDEN = 8192
WINDOW = 2048
PART = VD // 4
MARK_ROWS = 16

SEQ = ("zh", "zl", "x")
f32 = jnp.float32
bf16 = jnp.bfloat16


def halves(x):
    high = x.astype(bf16)
    return high, (x - high.astype(f32)).astype(bf16)


def dot(a, b, dims=((1,), (0,))):
    return lax.dot_general(a, b, (dims, ((), ())), preferred_element_type=f32)


def dot3(a, b):
    ah, al = halves(a)
    bh, bl = halves(b)
    return dot(ah, bh) + (dot(ah, bl) + dot(al, bh))


def dot2(a, b):
    ah, al = halves(a)
    return dot(ah, b) + dot(al, b)


def call(body, out_shape, scalars=0, inputs=1, scratch=(), flops=1e7, mib=8):
    whole = pl.BlockSpec(memory_space=pltpu.VMEM)
    small = pl.BlockSpec(memory_space=pltpu.SMEM)
    return pl.pallas_call(
        body,
        in_specs=[small] * scalars + [whole] * inputs,
        out_specs=jax.tree.map(lambda _: whole, out_shape),
        out_shape=out_shape,
        scratch_shapes=list(scratch),
        cost_estimate=pl.CostEstimate(flops=int(flops), bytes_accessed=10**6, transcendentals=0),
        compiler_params=pltpu.CompilerParams(vmem_limit_bytes=mib * 2**20),
    )


def block_terms(
    count_ref, q_ref, k_ref, v_ref, gate_ref, beta_ref, map_ref, carry_ref, local_ref, x_ref, a_ref
):
    count = count_ref[0]
    row = lax.broadcasted_iota(jnp.int32, (ROWS, ROWS), 0)
    col = lax.broadcasted_iota(jnp.int32, (ROWS, ROWS), 1)
    lane = lax.broadcasted_iota(jnp.int32, (1, ROWS), 1)
    eye = row == col
    kept = []
    for h in range(HEADS):
        k = k_ref[h]
        gate = jnp.where(lane < count, gate_ref[h : h + 1, :], 0.0)
        beta = jnp.where(lane < count, beta_ref[h : h + 1, :], 0.0)
        log_col = jnp.sum(jnp.where(col <= row, gate, 0.0), axis=1, keepdims=True)
        log_row = jnp.sum(jnp.where(eye, log_col, 0.0), axis=0, keepdims=True)
        beta_col = jnp.sum(jnp.where(eye, beta, 0.0), axis=1, keepdims=True)
        gram = dot(k, k, ((1,), (1,)))
        squares = jnp.where(eye, gram, 0.0)
        k_col = lax.rsqrt(jnp.sum(squares, axis=1, keepdims=True) + 1e-6)
        k_row = lax.rsqrt(jnp.sum(squares, axis=0, keepdims=True) + 1e-6)
        decay = jnp.where(col <= row, jnp.exp(jnp.minimum(log_col - log_row, 0.0)), 0.0)
        a = jnp.where(col < row, (beta_col * k_col) * decay * (gram * k_row), 0.0)
        a_ref[h] = a
        x_ref[h] = jnp.where(eye, 1.0, jnp.where((row >> 1) == (col >> 1), -a, 0.0))
        q = q_ref[h]
        wide = q.astype(f32)
        q_col = lax.rsqrt(jnp.sum(wide * wide, axis=1, keepdims=True) + 1e-6)
        local_ref[h] = (q_col * decay) * (dot(q, k, ((1,), (1,))) * k_row)
        kept.append((log_col, log_row, beta, k_col, k_row, q_col))
    step = 1
    while (2 << step) <= ROWS:
        m = 1 << step
        for h in range(HEADS):
            if m < 64:
                x = x_ref[h]
                below = ((row >> (step + 1)) == (col >> (step + 1))) & ((row >> step) != (col >> step))
                coarse = x.astype(bf16)
                between = jnp.where(below, a_ref[h], 0.0).astype(bf16)
                x_ref[h] = x - dot(dot(coarse, between).astype(bf16), coarse)
            else:
                for s in range(0, ROWS, 2 * m):
                    first = x_ref[h, s : s + m, s : s + m].astype(bf16)
                    second = x_ref[h, s + m : s + 2 * m, s + m : s + 2 * m].astype(bf16)
                    between = a_ref[h, s + m : s + 2 * m, s : s + m].astype(bf16)
                    x_ref[h, s + m : s + 2 * m, s : s + m] = -dot(
                        second, dot(between, first).astype(bf16)
                    )
        step += 1
    for h in range(HEADS):
        x = x_ref[h]
        left = jnp.where(eye, 1.0, 0.0) - x - dot3(a_ref[h], x)
        x_ref[h] = x + dot(x.astype(bf16), left.astype(bf16))
    row_k = lax.broadcasted_iota(jnp.int32, (KD, KD), 0)
    col_k = lax.broadcasted_iota(jnp.int32, (KD, KD), 1)
    for h in range(HEADS):
        log_col, log_row, beta, k_col, k_row, q_col = kept[h]
        k = k_ref[h]
        x = x_ref[h]
        new_value = dot2(x * beta, v_ref[h])
        new_key = dot2(x * (beta * jnp.exp(log_row) * k_row), k)
        new = jnp.concatenate([new_key, new_value], axis=1)
        last = log_col[ROWS - 1 : ROWS, :]
        high, low = halves((jnp.exp(last - log_col) * k_col) * new)
        update = dot(k, high, ((0,), (0,))) + dot(k, low, ((0,), (0,)))
        map_ref[h, :, :KD] = jnp.where(row_k == col_k, jnp.exp(last), 0.0) - update[:, :KD]
        map_ref[h, :, KD:] = update[:, KD:]
        mixed = dot3(local_ref[h], new)
        carry_ref[h] = (jnp.exp(log_col) * q_col) * q_ref[h].astype(f32) - mixed[:, :KD]
        local_ref[h] = mixed[:, KD:]


def fold(x):
    half = KD // 2
    return jnp.concatenate([x[:half, :], x[half:, :]], axis=1)


def unfold(x):
    return jnp.concatenate([x[:, :PART], x[:, PART:]], axis=0)


def then(state, transition, offset):
    state = dot3(transition, state)
    return jnp.concatenate([state[:, :KD], state[:, KD:] + offset], axis=1)


def compose_plane(maps_ref, before_ref, send_ref):
    state = maps_ref[0]
    for i in range(1, 4):
        before_ref[i - 1] = state
        state = then(state, maps_ref[i, :, :KD], maps_ref[i, :, KD:])
    for i in range(4):
        send_ref[i, :KD, :] = state[:, :KD]
        send_ref[i, KD:, :] = fold(state[:, KD + i * PART : KD + (i + 1) * PART])


def compose_group(maps_ref, before_ref, total_ref, offset_ref):
    state = jnp.concatenate([maps_ref[0, :KD, :], unfold(maps_ref[0, KD:, :])], axis=1)
    for i in range(1, 4):
        before_ref[i - 1] = state
        state = then(state, maps_ref[i, :KD, :], unfold(maps_ref[i, KD:, :]))
    offset = fold(state[:, KD:])
    total_ref[:KD, :] = state[:, :KD]
    total_ref[KD:, :] = offset
    offset_ref[...] = offset


def step_state(map_ref, earlier_ref, out_ref):
    state = dot3(map_ref[:KD, :], unfold(earlier_ref[...]))
    out_ref[...] = fold(state) + map_ref[KD:, :]


def group_states(place_ref, first_ref, one_ref, two_ref, third_ref, before_ref, out_ref):
    place = place_ref[0]
    last = fold(dot3(third_ref[:KD, :], unfold(two_ref[...]))) + third_ref[KD:, :]
    state = jnp.where(
        place == 0,
        0.0,
        jnp.where(place == 1, first_ref[...], jnp.where(place == 2, one_ref[...], last)),
    )
    out_ref[0] = state
    state = unfold(state)
    for i in range(3):
        out_ref[i + 1] = fold(dot3(before_ref[i, :, :KD], state) + before_ref[i, :, KD:])


def plane_states(parts_ref, before_ref, attn_ref, out_ref):
    state = jnp.concatenate([unfold(parts_ref[i]) for i in range(4)], axis=1)
    for i in range(4):
        entering = state
        if i > 0:
            entering = dot3(before_ref[i - 1, :, :KD], state) + before_ref[i - 1, :, KD:]
        out_ref[i, :KD, :], out_ref[i, KD : 2 * KD, :] = halves(entering)
        out_ref[i, 2 * KD :, :] = attn_ref[i]


def raw_rows(carry_ref, local_ref, state_ref, raw_ref, square_ref):
    total = jnp.zeros((ROWS, VD), f32)
    for h in range(HEADS):
        carry_high, carry_low = halves(carry_ref[h])
        high, low = state_ref[h, :KD, :], state_ref[h, KD : 2 * KD, :]
        raw = local_ref[h] + dot(carry_high, high) + (dot(carry_high, low) + dot(carry_low, high))
        raw_ref[h] = raw
        total = total + raw * raw
    column = jnp.sum(total, axis=1, keepdims=True)
    row = lax.broadcasted_iota(jnp.int32, (ROWS, ROWS), 0)
    col = lax.broadcasted_iota(jnp.int32, (ROWS, ROWS), 1)
    square_ref[...] = jnp.broadcast_to(
        jnp.sum(jnp.where(row == col, column, 0.0), axis=0, keepdims=True), square_ref.shape
    )


def normed(count_ref, raw_ref, square_ref, gain_ref, out_ref):
    row = lax.broadcasted_iota(jnp.int32, (ROWS, ROWS), 0)
    col = lax.broadcasted_iota(jnp.int32, (ROWS, ROWS), 1)
    total = square_ref[0:1, :]
    for i in range(1, 8):
        total = total + square_ref[8 * i : 8 * i + 1, :]
    column = jnp.sum(jnp.where(row == col, total, 0.0), axis=1, keepdims=True)
    live = lax.broadcasted_iota(jnp.int32, (ROWS, 1), 0) < count_ref[0]
    factor = jnp.where(live, lax.rsqrt(column * (1.0 / HIDDEN) + 1e-6), 0.0)
    for h in range(HEADS):
        out_ref[h] = (raw_ref[h] * factor * gain_ref[h : h + 1, :]).astype(bf16)


def pack_blocks(count_ref, key_ref, value_ref, query_ref, position_ref, out_ref):
    lane = lax.broadcasted_iota(jnp.int32, (1, ROWS), 1)
    marks = jnp.where(lane < count_ref[0], position_ref[...] + 1, 0)
    spot = lax.broadcasted_iota(jnp.int32, (MARK_ROWS, ROWS), 0)
    coded = jnp.where(spot == 0, marks >> 8, jnp.where(spot == 1, marks & 255, 0))
    coded = coded.astype(f32).astype(bf16)
    for h in range(HEADS):
        out_ref[h, :ROWS, :KD] = key_ref[h]
        out_ref[h, :ROWS, KD : KD + VD] = value_ref[h]
        out_ref[h, :ROWS, KD + VD :] = query_ref[h]
        out_ref[h, ROWS:, :ROWS] = coded
        out_ref[h, ROWS:, ROWS:] = jnp.zeros((MARK_ROWS, 2 * KD + VD - ROWS), bf16)


def attend(here_ref, past_ref, out_ref):
    row = lax.broadcasted_iota(jnp.int32, (ROWS, ROWS), 0)
    col = lax.broadcasted_iota(jnp.int32, (ROWS, ROWS), 1)

    def marks_of(ref, j):
        coded = ref[j, ROWS : ROWS + MARK_ROWS, :ROWS].astype(f32)
        return coded[0:1, :] * 256.0 + coded[1:2, :]

    marks = [marks_of(here_ref, j) for j in range(4)]
    here_marks = [jnp.where(m > 0.0, m, 1e9) for m in marks]
    past_marks = [marks_of(past_ref, j) for j in range(4)]
    past_marks = [jnp.where(m > 0.0, m, 1e9) for m in past_marks]
    for j in range(4):
        query_marks = jnp.sum(jnp.where(row == col, marks[j], 0.0), axis=1, keepdims=True)
        q = here_ref[j, :ROWS, KD + VD :]
        sources = [(here_ref, i, here_marks[i]) for i in range(j + 1)]
        sources += [(past_ref, i, past_marks[i]) for i in range(j, 4)]
        scores = []
        for ref, i, key_marks in sources:
            score = dot(q, ref[i, :ROWS, :KD], ((1,), (1,))) * KD**-0.5
            allowed = (key_marks <= query_marks) & (key_marks > query_marks - float(WINDOW))
            scores.append(jnp.where(allowed, score, -1e30))
        top = scores[0]
        for score in scores[1:]:
            top = jnp.maximum(top, score)
        top = jnp.max(top, axis=1, keepdims=True)
        weight_sum = jnp.zeros((ROWS, ROWS), f32)
        mixed = jnp.zeros((ROWS, VD), f32)
        for score, (ref, i, key_marks) in zip(scores, sources):
            weights = jnp.exp(score - top)
            weight_sum = weight_sum + weights
            mixed = mixed + dot(weights.astype(bf16), ref[i, :ROWS, KD : KD + VD])
        mixed = mixed / jnp.sum(weight_sum, axis=1, keepdims=True)
        out_ref[j] = jnp.where(query_marks > 0.0, mixed, 0.0).astype(bf16)


def heads_first(block):
    return jnp.swapaxes(block, 0, 1)


def shape_of(*dims, kind=f32):
    return jax.ShapeDtypeStruct(dims, kind)


def shards(
    delta_query,
    delta_key,
    delta_value,
    delta_gate,
    delta_beta,
    delta_count,
    delta_gain,
    attn_query,
    attn_key,
    attn_value,
    attn_position,
    attn_count,
):
    packed = call(
        pack_blocks, shape_of(HEADS, ROWS + MARK_ROWS, 2 * KD + VD, kind=bf16), scalars=1, inputs=4
    )(
        attn_count,
        heads_first(attn_key),
        heads_first(attn_value),
        heads_first(attn_query),
        attn_position.reshape(1, ROWS),
    )
    here = lax.all_to_all(packed, "x", 0, 0, tiled=True)
    maps, carry, local = call(
        block_terms,
        (shape_of(HEADS, KD, KD + VD), shape_of(HEADS, ROWS, KD), shape_of(HEADS, ROWS, VD)),
        scalars=1,
        inputs=5,
        scratch=[pltpu.VMEM((HEADS, ROWS, ROWS), f32)] * 2,
        flops=8e9,
        mib=16,
    )(
        delta_count,
        heads_first(delta_query),
        heads_first(delta_key),
        heads_first(delta_value),
        delta_gate.T,
        delta_beta.T,
    )
    maps, here = lax.optimization_barrier((maps, here))
    past = lax.ppermute(here[:, :, : KD + VD], ("zh", "zl"), [(i, i + 1) for i in range(15)])
    exchanged = lax.all_to_all(maps, "x", 0, 0, tiled=True)
    plane_prefix, plane_total = call(
        compose_plane, (shape_of(3, KD, KD + VD), shape_of(4, KD + PART, KD))
    )(exchanged)
    gathered = lax.all_to_all(plane_total, "zl", 0, 0, tiled=True)
    group_prefix, group_total, group_offset = call(
        compose_group,
        (shape_of(3, KD, KD + PART), shape_of(KD + PART, KD), shape_of(PART, KD)),
    )(gathered)
    first = lax.ppermute(group_offset, "zh", [(0, 1)])
    third = lax.ppermute(group_total, "zh", [(2, 3)])
    pair = call(step_state, shape_of(PART, KD), inputs=2)(group_total, first)
    one = lax.ppermute(pair, "zh", [(1, 2)])
    two = lax.ppermute(pair, "zh", [(1, 3)])
    place = lax.axis_index("zh").astype(jnp.int32).reshape(1)
    planes = call(group_states, shape_of(4, PART, KD), scalars=1, inputs=5)(
        place, first, one, two, third, group_prefix
    )
    planes, past = lax.optimization_barrier((planes, past))
    attn_heads = call(attend, shape_of(4, ROWS, VD, kind=bf16), inputs=2, flops=8e9, mib=16)(here, past)
    parts = lax.all_to_all(planes, "zl", 0, 0, tiled=True)
    returned = call(plane_states, shape_of(4, 2 * KD + ROWS, VD, kind=bf16), inputs=3)(
        parts, plane_prefix, attn_heads
    )
    states = lax.all_to_all(returned, "x", 0, 0, tiled=True)
    raw, squares = call(
        raw_rows, (shape_of(HEADS, ROWS, VD), shape_of(64, ROWS)), inputs=3
    )(carry, local, states)
    squares = lax.all_to_all(squares, "head", 0, 0, tiled=True)
    delta_heads = call(normed, shape_of(HEADS, ROWS, VD, kind=bf16), scalars=1, inputs=3)(
        delta_count, raw, squares, delta_gain
    )
    return (heads_first(delta_heads), heads_first(states[:, 2 * KD :]))


def solution(mesh):
    grid = Mesh(mesh.devices.reshape(4, 4, 4, 8), SEQ + ("head",))
    rows = P(SEQ, "head", None)
    pairs = P(SEQ, "head")
    block = P(SEQ)
    return jax.shard_map(
        shards,
        mesh=grid,
        in_specs=(rows, rows, rows, pairs, pairs, block, P("head", None), rows, rows, rows, block, block),
        out_specs=(rows, rows),
        check_vma=False,
    )
```

```python
import jax
import jax.numpy as jnp
from jax import lax
from jax.experimental import pallas as pl
from jax.experimental.pallas import tpu as pltpu
from jax.sharding import Mesh, PartitionSpec as P

ROWS = 256
KD = 128
VD = 256
HEADS = 4
HIDDEN = 8192
WINDOW = 2048
PART = VD // 4
MARK_ROWS = 16
BEFORE = 2 * KD + VD

SEQ = ("zh", "zl", "x")
f32 = jnp.float32
bf16 = jnp.bfloat16


def halves(x):
    high = x.astype(bf16)
    return high, (x - high.astype(f32)).astype(bf16)


def dot(a, b, dims=((1,), (0,))):
    return lax.dot_general(a, b, (dims, ((), ())), preferred_element_type=f32)


def dot3(a, b):
    ah, al = halves(a)
    bh, bl = halves(b)
    return dot(ah, bh) + (dot(ah, bl) + dot(al, bh))


def dot2(a, b):
    ah, al = halves(a)
    return dot(ah, b) + dot(al, b)


def call(body, out_shape, scalars=0, inputs=1, scratch=(), flops=1e7, mib=8):
    whole = pl.BlockSpec(memory_space=pltpu.VMEM)
    small = pl.BlockSpec(memory_space=pltpu.SMEM)
    return pl.pallas_call(
        body,
        in_specs=[small] * scalars + [whole] * inputs,
        out_specs=jax.tree.map(lambda _: whole, out_shape),
        out_shape=out_shape,
        scratch_shapes=list(scratch),
        cost_estimate=pl.CostEstimate(flops=int(flops), bytes_accessed=10**6, transcendentals=0),
        compiler_params=pltpu.CompilerParams(vmem_limit_bytes=mib * 2**20),
    )


def block_terms(
    count_ref, q_ref, k_ref, v_ref, gate_ref, beta_ref, map_ref, carry_ref, local_ref, x_ref, a_ref
):
    count = count_ref[0]
    row = lax.broadcasted_iota(jnp.int32, (ROWS, ROWS), 0)
    col = lax.broadcasted_iota(jnp.int32, (ROWS, ROWS), 1)
    lane = lax.broadcasted_iota(jnp.int32, (1, ROWS), 1)
    eye = row == col
    kept = []
    for h in range(HEADS):
        k = k_ref[h]
        gate = jnp.where(lane < count, gate_ref[h : h + 1, :], 0.0)
        beta = jnp.where(lane < count, beta_ref[h : h + 1, :], 0.0)
        log_col = jnp.sum(jnp.where(col <= row, gate, 0.0), axis=1, keepdims=True)
        log_row = jnp.sum(jnp.where(eye, log_col, 0.0), axis=0, keepdims=True)
        beta_col = jnp.sum(jnp.where(eye, beta, 0.0), axis=1, keepdims=True)
        gram = dot(k, k, ((1,), (1,)))
        squares = jnp.where(eye, gram, 0.0)
        k_col = lax.rsqrt(jnp.sum(squares, axis=1, keepdims=True) + 1e-6)
        k_row = lax.rsqrt(jnp.sum(squares, axis=0, keepdims=True) + 1e-6)
        decay = jnp.where(col <= row, jnp.exp(jnp.minimum(log_col - log_row, 0.0)), 0.0)
        a = jnp.where(col < row, (beta_col * k_col) * decay * (gram * k_row), 0.0)
        a_ref[h] = a
        x_ref[h] = jnp.where(eye, 1.0, jnp.where((row >> 1) == (col >> 1), -a, 0.0))
        q = q_ref[h]
        wide = q.astype(f32)
        q_col = lax.rsqrt(jnp.sum(wide * wide, axis=1, keepdims=True) + 1e-6)
        local_ref[h] = (q_col * decay) * (dot(q, k, ((1,), (1,))) * k_row)
        kept.append((log_col, log_row, beta, k_col, k_row, q_col))
    step = 1
    while (2 << step) <= ROWS:
        m = 1 << step
        for h in range(HEADS):
            if m < 64:
                x = x_ref[h]
                below = ((row >> (step + 1)) == (col >> (step + 1))) & ((row >> step) != (col >> step))
                coarse = x.astype(bf16)
                between = jnp.where(below, a_ref[h], 0.0).astype(bf16)
                x_ref[h] = x - dot(dot(coarse, between).astype(bf16), coarse)
            else:
                for s in range(0, ROWS, 2 * m):
                    first = x_ref[h, s : s + m, s : s + m].astype(bf16)
                    second = x_ref[h, s + m : s + 2 * m, s + m : s + 2 * m].astype(bf16)
                    between = a_ref[h, s + m : s + 2 * m, s : s + m].astype(bf16)
                    x_ref[h, s + m : s + 2 * m, s : s + m] = -dot(
                        second, dot(between, first).astype(bf16)
                    )
        step += 1
    for h in range(HEADS):
        x = x_ref[h]
        left = jnp.where(eye, 1.0, 0.0) - x - dot3(a_ref[h], x)
        x_ref[h] = x + dot(x.astype(bf16), left.astype(bf16))
    row_k = lax.broadcasted_iota(jnp.int32, (KD, KD), 0)
    col_k = lax.broadcasted_iota(jnp.int32, (KD, KD), 1)
    for h in range(HEADS):
        log_col, log_row, beta, k_col, k_row, q_col = kept[h]
        k = k_ref[h]
        x = x_ref[h]
        new_value = dot2(x * beta, v_ref[h])
        new_key = dot2(x * (beta * jnp.exp(log_row) * k_row), k)
        new = jnp.concatenate([new_key, new_value], axis=1)
        last = log_col[ROWS - 1 : ROWS, :]
        high, low = halves((jnp.exp(last - log_col) * k_col) * new)
        update = dot(k, high, ((0,), (0,))) + dot(k, low, ((0,), (0,)))
        map_ref[h, :, :KD] = jnp.where(row_k == col_k, jnp.exp(last), 0.0) - update[:, :KD]
        map_ref[h, :, KD:] = update[:, KD:]
        mixed = dot3(local_ref[h], new)
        carry_ref[h] = (jnp.exp(log_col) * q_col) * q_ref[h].astype(f32) - mixed[:, :KD]
        local_ref[h] = mixed[:, KD:]


def fold(x):
    half = KD // 2
    return jnp.concatenate([x[:half, :], x[half:, :]], axis=1)


def unfold(x):
    return jnp.concatenate([x[:, :PART], x[:, PART:]], axis=0)


def then(state, transition, offset):
    state = dot3(transition, state)
    return jnp.concatenate([state[:, :KD], state[:, KD:] + offset], axis=1)


def pick(index, choices):
    picked = choices[0]
    for i in range(1, len(choices)):
        picked = jnp.where(index == i, choices[i], picked)
    return picked


def ahead(place, shift):
    return lax.rem(place + shift, 4)


def compose_plane(place_ref, maps_ref, before_ref, *send_refs):
    state = maps_ref[0]
    for i in range(1, 4):
        before_ref[i - 1] = state
        state = then(state, maps_ref[i, :, :KD], maps_ref[i, :, KD:])
    quarters = [fold(state[:, KD + i * PART : KD + (i + 1) * PART]) for i in range(4)]
    for d, send_ref in enumerate(send_refs):
        send_ref[:KD, :] = state[:, :KD]
        send_ref[KD:, :] = pick(ahead(place_ref[0], d), quarters)


def in_order(place, refs, ordered_ref):
    for d, ref in enumerate(refs):
        ordered_ref[pl.ds(ahead(place, 4 - d), 1)] = ref[...][None]


def compose_group(
    place_ref, own_ref, one_ref, two_ref, three_ref, before_ref, total_ref, offset_ref, maps_ref
):
    in_order(place_ref[0], (own_ref, one_ref, two_ref, three_ref), maps_ref)
    state = jnp.concatenate([maps_ref[0, :KD, :], unfold(maps_ref[0, KD:, :])], axis=1)
    for i in range(1, 4):
        before_ref[i - 1] = state
        state = then(state, maps_ref[i, :KD, :], unfold(maps_ref[i, KD:, :]))
    offset = fold(state[:, KD:])
    total_ref[:KD, :] = state[:, :KD]
    total_ref[KD:, :] = offset
    offset_ref[...] = offset


def step_state(map_ref, earlier_ref, out_ref):
    state = dot3(map_ref[:KD, :], unfold(earlier_ref[...]))
    out_ref[...] = fold(state) + map_ref[KD:, :]


def group_states(place_ref, first_ref, one_ref, two_ref, third_ref, before_ref, out_ref):
    place = place_ref[0]
    last = fold(dot3(third_ref[:KD, :], unfold(two_ref[...]))) + third_ref[KD:, :]
    state = jnp.where(
        place == 0,
        0.0,
        jnp.where(place == 1, first_ref[...], jnp.where(place == 2, one_ref[...], last)),
    )
    out_ref[0] = state
    state = unfold(state)
    for i in range(3):
        out_ref[i + 1] = fold(dot3(before_ref[i, :, :KD], state) + before_ref[i, :, KD:])


def plane_states(parts_ref, before_ref, attn_ref, out_ref):
    state = jnp.concatenate([unfold(parts_ref[i]) for i in range(4)], axis=1)
    for i in range(4):
        entering = state
        if i > 0:
            entering = dot3(before_ref[i - 1, :, :KD], state) + before_ref[i - 1, :, KD:]
        out_ref[i, :KD, :], out_ref[i, KD : 2 * KD, :] = halves(entering)
        out_ref[i, 2 * KD :, :] = attn_ref[i]


def raw_rows(carry_ref, local_ref, state_ref, raw_ref, square_ref):
    total = jnp.zeros((ROWS, VD), f32)
    for h in range(HEADS):
        carry_high, carry_low = halves(carry_ref[h])
        high, low = state_ref[h, :KD, :], state_ref[h, KD : 2 * KD, :]
        raw = local_ref[h] + dot(carry_high, high) + (dot(carry_high, low) + dot(carry_low, high))
        raw_ref[h] = raw
        total = total + raw * raw
    column = jnp.sum(total, axis=1, keepdims=True)
    row = lax.broadcasted_iota(jnp.int32, (ROWS, ROWS), 0)
    col = lax.broadcasted_iota(jnp.int32, (ROWS, ROWS), 1)
    square_ref[...] = jnp.broadcast_to(
        jnp.sum(jnp.where(row == col, column, 0.0), axis=0, keepdims=True), square_ref.shape
    )


def normed(count_ref, raw_ref, square_ref, gain_ref, out_ref):
    row = lax.broadcasted_iota(jnp.int32, (ROWS, ROWS), 0)
    col = lax.broadcasted_iota(jnp.int32, (ROWS, ROWS), 1)
    total = square_ref[0:1, :]
    for i in range(1, 8):
        total = total + square_ref[8 * i : 8 * i + 1, :]
    column = jnp.sum(jnp.where(row == col, total, 0.0), axis=1, keepdims=True)
    live = lax.broadcasted_iota(jnp.int32, (ROWS, 1), 0) < count_ref[0]
    factor = jnp.where(live, lax.rsqrt(column * (1.0 / HIDDEN) + 1e-6), 0.0)
    for h in range(HEADS):
        out_ref[h] = (raw_ref[h] * factor * gain_ref[h : h + 1, :]).astype(bf16)


def pack_keys(count_ref, key_ref, value_ref, position_ref, out_ref):
    lane = lax.broadcasted_iota(jnp.int32, (1, ROWS), 1)
    marks = jnp.where(lane < count_ref[0], position_ref[...] + 1, 0)
    spot = lax.broadcasted_iota(jnp.int32, (MARK_ROWS, ROWS), 0)
    coded = jnp.where(spot == 0, marks >> 8, jnp.where(spot == 1, marks & 255, 0))
    coded = coded.astype(f32).astype(bf16)
    for h in range(HEADS):
        out_ref[h, :ROWS, :KD] = key_ref[h]
        out_ref[h, :ROWS, KD:] = value_ref[h]
        out_ref[h, ROWS:, :ROWS] = coded
        out_ref[h, ROWS:, ROWS:] = jnp.zeros((MARK_ROWS, KD + VD - ROWS), bf16)


def pack_heads(query_ref, keys_ref, past_ref, out_ref):
    for h in range(HEADS):
        out_ref[h, :, : KD + VD] = keys_ref[h]
        out_ref[h, :ROWS, KD + VD : BEFORE] = query_ref[h]
        out_ref[h, ROWS:, KD + VD : BEFORE] = jnp.zeros((MARK_ROWS, KD), bf16)
        out_ref[h, :, BEFORE:] = past_ref[h]


def attend(blocks_ref, out_ref):
    row = lax.broadcasted_iota(jnp.int32, (ROWS, ROWS), 0)
    col = lax.broadcasted_iota(jnp.int32, (ROWS, ROWS), 1)

    def marks_of(start, j):
        coded = blocks_ref[j, ROWS : ROWS + MARK_ROWS, start : start + ROWS].astype(f32)
        return coded[0:1, :] * 256.0 + coded[1:2, :]

    marks = [marks_of(0, j) for j in range(4)]
    here_marks = [jnp.where(m > 0.0, m, 1e9) for m in marks]
    past_marks = [marks_of(BEFORE, j) for j in range(4)]
    past_marks = [jnp.where(m > 0.0, m, 1e9) for m in past_marks]
    for j in range(4):
        query_marks = jnp.sum(jnp.where(row == col, marks[j], 0.0), axis=1, keepdims=True)
        q = blocks_ref[j, :ROWS, KD + VD : BEFORE]
        sources = [(0, i, here_marks[i]) for i in range(j + 1)]
        sources += [(BEFORE, i, past_marks[i]) for i in range(j, 4)]
        scores = []
        for start, i, key_marks in sources:
            score = dot(q, blocks_ref[i, :ROWS, start : start + KD], ((1,), (1,))) * KD**-0.5
            allowed = (key_marks <= query_marks) & (key_marks > query_marks - float(WINDOW))
            scores.append(jnp.where(allowed, score, -1e30))
        top = scores[0]
        for score in scores[1:]:
            top = jnp.maximum(top, score)
        top = jnp.max(top, axis=1, keepdims=True)
        weight_sum = jnp.zeros((ROWS, ROWS), f32)
        mixed = jnp.zeros((ROWS, VD), f32)
        for score, (start, i, key_marks) in zip(scores, sources):
            weights = jnp.exp(score - top)
            weight_sum = weight_sum + weights
            values = blocks_ref[i, :ROWS, start + KD : start + KD + VD]
            mixed = mixed + dot(weights.astype(bf16), values)
        mixed = mixed / jnp.sum(weight_sum, axis=1, keepdims=True)
        out_ref[j] = jnp.where(query_marks > 0.0, mixed, 0.0).astype(bf16)


def heads_first(block):
    return jnp.swapaxes(block, 0, 1)


def around(parts, axis):
    return [
        lax.ppermute(part, axis, [(i, (i + d) % 4) for i in range(4)]) if d else part
        for d, part in enumerate(parts)
    ]


def shape_of(*dims, kind=f32):
    return jax.ShapeDtypeStruct(dims, kind)


def shards(
    delta_query,
    delta_key,
    delta_value,
    delta_gate,
    delta_beta,
    delta_count,
    delta_gain,
    attn_query,
    attn_key,
    attn_value,
    attn_position,
    attn_count,
):
    keys = call(
        pack_keys, shape_of(HEADS, ROWS + MARK_ROWS, KD + VD, kind=bf16), scalars=1, inputs=3
    )(attn_count, heads_first(attn_key), heads_first(attn_value), attn_position.reshape(1, ROWS))
    past = lax.ppermute(keys, ("zh", "zl"), [(i, i + 1) for i in range(15)])
    maps, carry, local = call(
        block_terms,
        (shape_of(HEADS, KD, KD + VD), shape_of(HEADS, ROWS, KD), shape_of(HEADS, ROWS, VD)),
        scalars=1,
        inputs=5,
        scratch=[pltpu.VMEM((HEADS, ROWS, ROWS), f32)] * 2,
        flops=8e9,
        mib=16,
    )(
        delta_count,
        heads_first(delta_query),
        heads_first(delta_key),
        heads_first(delta_value),
        delta_gate.T,
        delta_beta.T,
    )
    maps, attn_query = lax.optimization_barrier((maps, attn_query))
    exchanged = lax.all_to_all(maps, "x", 0, 0, tiled=True)
    packed = call(
        pack_heads, shape_of(HEADS, ROWS + MARK_ROWS, BEFORE + KD + VD, kind=bf16), inputs=3
    )(heads_first(attn_query), keys, past)
    exchanged, packed = lax.optimization_barrier((exchanged, packed))
    zl = lax.axis_index("zl").astype(jnp.int32).reshape(1)
    plane_prefix, *plane_totals = call(
        compose_plane,
        (shape_of(3, KD, KD + VD),) + (shape_of(KD + PART, KD),) * 4,
        scalars=1,
    )(zl, exchanged)
    _, packed = lax.optimization_barrier((plane_totals[0], packed))
    blocks = lax.all_to_all(packed, "x", 0, 0, tiled=True)
    group_prefix, group_total, group_offset = call(
        compose_group,
        (shape_of(3, KD, KD + PART), shape_of(KD + PART, KD), shape_of(PART, KD)),
        scalars=1,
        inputs=4,
        scratch=[pltpu.VMEM((4, KD + PART, KD), f32)],
    )(zl, *around(plane_totals, "zl"))
    first = lax.ppermute(group_offset, "zh", [(0, 1)])
    third = lax.ppermute(group_total, "zh", [(2, 3)])
    pair = call(step_state, shape_of(PART, KD), inputs=2)(group_total, first)
    one = lax.ppermute(pair, "zh", [(1, 2)])
    two = lax.ppermute(pair, "zh", [(1, 3)])
    place = lax.axis_index("zh").astype(jnp.int32).reshape(1)
    planes = call(group_states, shape_of(4, PART, KD), scalars=1, inputs=5)(
        place, first, one, two, third, group_prefix
    )
    planes, blocks = lax.optimization_barrier((planes, blocks))
    attn_heads = call(attend, shape_of(4, ROWS, VD, kind=bf16), flops=8e9, mib=16)(blocks)
    parts = lax.all_to_all(planes, "zl", 0, 0, tiled=True)
    returned = call(plane_states, shape_of(4, 2 * KD + ROWS, VD, kind=bf16), inputs=3)(
        parts, plane_prefix, attn_heads
    )
    states = lax.all_to_all(returned, "x", 0, 0, tiled=True)
    raw, squares = call(
        raw_rows, (shape_of(HEADS, ROWS, VD), shape_of(64, ROWS)), inputs=3
    )(carry, local, states)
    squares = lax.all_to_all(squares, "head", 0, 0, tiled=True)
    delta_heads = call(normed, shape_of(HEADS, ROWS, VD, kind=bf16), scalars=1, inputs=3)(
        delta_count, raw, squares, delta_gain
    )
    return (heads_first(delta_heads), heads_first(states[:, 2 * KD :]))


def solution(mesh):
    grid = Mesh(mesh.devices.reshape(4, 4, 4, 8), SEQ + ("head",))
    rows = P(SEQ, "head", None)
    pairs = P(SEQ, "head")
    block = P(SEQ)
    return jax.shard_map(
        shards,
        mesh=grid,
        in_specs=(rows, rows, rows, pairs, pairs, block, P("head", None), rows, rows, rows, block, block),
        out_specs=(rows, rows),
        check_vma=False,
    )
```

```python
import jax
import jax.numpy as jnp
from jax import lax
from jax.experimental import pallas as pl
from jax.experimental.pallas import tpu as pltpu
from jax.sharding import Mesh, PartitionSpec as P

ROWS = 256
KD = 128
VD = 256
HEADS = 4
HIDDEN = 8192
WINDOW = 2048
PART = VD // 4
MARK_ROWS = 16
BEFORE = 2 * KD + VD

SEQ = ("zh", "zl", "x")
f32 = jnp.float32
bf16 = jnp.bfloat16


def halves(x):
    high = x.astype(bf16)
    return high, (x - high.astype(f32)).astype(bf16)


def dot(a, b, dims=((1,), (0,))):
    return lax.dot_general(a, b, (dims, ((), ())), preferred_element_type=f32)


def dot3(a, b):
    ah, al = halves(a)
    bh, bl = halves(b)
    return dot(ah, bh) + (dot(ah, bl) + dot(al, bh))


def dot2(a, b):
    ah, al = halves(a)
    return dot(ah, b) + dot(al, b)


def call(body, out_shape, scalars=0, inputs=1, scratch=(), flops=1e7, mib=8):
    whole = pl.BlockSpec(memory_space=pltpu.VMEM)
    small = pl.BlockSpec(memory_space=pltpu.SMEM)
    return pl.pallas_call(
        body,
        in_specs=[small] * scalars + [whole] * inputs,
        out_specs=jax.tree.map(lambda _: whole, out_shape),
        out_shape=out_shape,
        scratch_shapes=list(scratch),
        cost_estimate=pl.CostEstimate(flops=int(flops), bytes_accessed=10**6, transcendentals=0),
        compiler_params=pltpu.CompilerParams(vmem_limit_bytes=mib * 2**20),
    )


def block_terms(
    count_ref, q_ref, k_ref, v_ref, gate_ref, beta_ref, map_ref, carry_ref, local_ref, x_ref, a_ref
):
    count = count_ref[0]
    row = lax.broadcasted_iota(jnp.int32, (ROWS, ROWS), 0)
    col = lax.broadcasted_iota(jnp.int32, (ROWS, ROWS), 1)
    lane = lax.broadcasted_iota(jnp.int32, (1, ROWS), 1)
    eye = row == col
    kept = []
    for h in range(HEADS):
        k = k_ref[h]
        gate = jnp.where(lane < count, gate_ref[h : h + 1, :], 0.0)
        beta = jnp.where(lane < count, beta_ref[h : h + 1, :], 0.0)
        log_col = jnp.sum(jnp.where(col <= row, gate, 0.0), axis=1, keepdims=True)
        log_row = jnp.sum(jnp.where(eye, log_col, 0.0), axis=0, keepdims=True)
        beta_col = jnp.sum(jnp.where(eye, beta, 0.0), axis=1, keepdims=True)
        gram = dot(k, k, ((1,), (1,)))
        squares = jnp.where(eye, gram, 0.0)
        k_col = lax.rsqrt(jnp.sum(squares, axis=1, keepdims=True) + 1e-6)
        k_row = lax.rsqrt(jnp.sum(squares, axis=0, keepdims=True) + 1e-6)
        decay = jnp.where(col <= row, jnp.exp(jnp.minimum(log_col - log_row, 0.0)), 0.0)
        a = jnp.where(col < row, (beta_col * k_col) * decay * (gram * k_row), 0.0)
        a_ref[h] = a
        x_ref[h] = jnp.where(eye, 1.0, jnp.where((row >> 1) == (col >> 1), -a, 0.0))
        q = q_ref[h]
        wide = q.astype(f32)
        q_col = lax.rsqrt(jnp.sum(wide * wide, axis=1, keepdims=True) + 1e-6)
        local_ref[h] = (q_col * decay) * (dot(q, k, ((1,), (1,))) * k_row)
        kept.append((log_col, log_row, beta, k_col, k_row, q_col))
    step = 1
    while (2 << step) <= ROWS:
        m = 1 << step
        for h in range(HEADS):
            if m < 64:
                x = x_ref[h]
                below = ((row >> (step + 1)) == (col >> (step + 1))) & ((row >> step) != (col >> step))
                coarse = x.astype(bf16)
                between = jnp.where(below, a_ref[h], 0.0).astype(bf16)
                x_ref[h] = x - dot(dot(coarse, between).astype(bf16), coarse)
            else:
                for s in range(0, ROWS, 2 * m):
                    first = x_ref[h, s : s + m, s : s + m].astype(bf16)
                    second = x_ref[h, s + m : s + 2 * m, s + m : s + 2 * m].astype(bf16)
                    between = a_ref[h, s + m : s + 2 * m, s : s + m].astype(bf16)
                    x_ref[h, s + m : s + 2 * m, s : s + m] = -dot(
                        second, dot(between, first).astype(bf16)
                    )
        step += 1
    for h in range(HEADS):
        x = x_ref[h]
        left = jnp.where(eye, 1.0, 0.0) - x - dot3(a_ref[h], x)
        x_ref[h] = x + dot(x.astype(bf16), left.astype(bf16))
    row_k = lax.broadcasted_iota(jnp.int32, (KD, KD), 0)
    col_k = lax.broadcasted_iota(jnp.int32, (KD, KD), 1)
    for h in range(HEADS):
        log_col, log_row, beta, k_col, k_row, q_col = kept[h]
        k = k_ref[h]
        x = x_ref[h]
        new_value = dot2(x * beta, v_ref[h])
        new_key = dot2(x * (beta * jnp.exp(log_row) * k_row), k)
        new = jnp.concatenate([new_key, new_value], axis=1)
        last = log_col[ROWS - 1 : ROWS, :]
        high, low = halves((jnp.exp(last - log_col) * k_col) * new)
        update = dot(k, high, ((0,), (0,))) + dot(k, low, ((0,), (0,)))
        transition = jnp.where(row_k == col_k, jnp.exp(last), 0.0) - update[:, :KD]
        map_ref[h, :, :KD], map_ref[h, :, KD : 2 * KD] = halves(transition)
        map_ref[h, :, 2 * KD :] = update[:, KD:].astype(bf16)
        mixed = dot3(local_ref[h], new)
        carry_ref[h] = (jnp.exp(log_col) * q_col) * q_ref[h].astype(f32) - mixed[:, :KD]
        local_ref[h] = mixed[:, KD:]


def fold(x):
    half = KD // 2
    return jnp.concatenate([x[:half, :], x[half:, :]], axis=1)


def unfold(x):
    return jnp.concatenate([x[:, :PART], x[:, PART:]], axis=0)


def then(state, transition, offset):
    state = dot3(transition, state)
    return jnp.concatenate([state[:, :KD], state[:, KD:] + offset], axis=1)


def compose_plane(maps_ref, before_ref, send_ref):
    def map_of(i):
        wide = maps_ref[i].astype(f32)
        return wide[:, :KD] + wide[:, KD : 2 * KD], wide[:, 2 * KD :]

    state = jnp.concatenate(map_of(0), axis=1)
    for i in range(1, 4):
        before_ref[i - 1] = state
        state = then(state, *map_of(i))
    for i in range(4):
        send_ref[i, :KD, :] = state[:, :KD]
        send_ref[i, KD:, :] = fold(state[:, KD + i * PART : KD + (i + 1) * PART])


def compose_group(maps_ref, before_ref, total_ref, offset_ref):
    state = jnp.concatenate([maps_ref[0, :KD, :], unfold(maps_ref[0, KD:, :])], axis=1)
    for i in range(1, 4):
        before_ref[i - 1] = state
        state = then(state, maps_ref[i, :KD, :], unfold(maps_ref[i, KD:, :]))
    offset = fold(state[:, KD:])
    total_ref[:KD, :] = state[:, :KD]
    total_ref[KD:, :] = offset
    offset_ref[...] = offset


def step_state(map_ref, earlier_ref, out_ref):
    state = dot3(map_ref[:KD, :], unfold(earlier_ref[...]))
    out_ref[...] = fold(state) + map_ref[KD:, :]


def group_states(place_ref, first_ref, one_ref, two_ref, third_ref, before_ref, out_ref):
    place = place_ref[0]
    last = fold(dot3(third_ref[:KD, :], unfold(two_ref[...]))) + third_ref[KD:, :]
    state = jnp.where(
        place == 0,
        0.0,
        jnp.where(place == 1, first_ref[...], jnp.where(place == 2, one_ref[...], last)),
    )
    out_ref[0] = state
    state = unfold(state)
    for i in range(3):
        out_ref[i + 1] = fold(dot3(before_ref[i, :, :KD], state) + before_ref[i, :, KD:])


def plane_states(parts_ref, before_ref, attn_ref, out_ref):
    state = jnp.concatenate([unfold(parts_ref[i]) for i in range(4)], axis=1)
    for i in range(4):
        entering = state
        if i > 0:
            entering = dot3(before_ref[i - 1, :, :KD], state) + before_ref[i - 1, :, KD:]
        out_ref[i, :KD, :] = entering.astype(bf16)
        out_ref[i, KD:, :] = attn_ref[i]


def raw_rows(carry_ref, local_ref, state_ref, raw_ref, square_ref):
    total = jnp.zeros((ROWS, VD), f32)
    for h in range(HEADS):
        raw = local_ref[h] + dot2(carry_ref[h], state_ref[h, :KD, :])
        raw_ref[h] = raw
        total = total + raw * raw
    column = jnp.sum(total, axis=1, keepdims=True)
    row = lax.broadcasted_iota(jnp.int32, (ROWS, ROWS), 0)
    col = lax.broadcasted_iota(jnp.int32, (ROWS, ROWS), 1)
    square_ref[...] = jnp.broadcast_to(
        jnp.sum(jnp.where(row == col, column, 0.0), axis=0, keepdims=True), square_ref.shape
    )


def normed(count_ref, raw_ref, square_ref, gain_ref, out_ref):
    row = lax.broadcasted_iota(jnp.int32, (ROWS, ROWS), 0)
    col = lax.broadcasted_iota(jnp.int32, (ROWS, ROWS), 1)
    total = square_ref[0:1, :]
    for i in range(1, 8):
        total = total + square_ref[8 * i : 8 * i + 1, :]
    column = jnp.sum(jnp.where(row == col, total, 0.0), axis=1, keepdims=True)
    live = lax.broadcasted_iota(jnp.int32, (ROWS, 1), 0) < count_ref[0]
    factor = jnp.where(live, lax.rsqrt(column * (1.0 / HIDDEN) + 1e-6), 0.0)
    for h in range(HEADS):
        out_ref[h] = (raw_ref[h] * factor * gain_ref[h : h + 1, :]).astype(bf16)


def pack_keys(count_ref, key_ref, value_ref, position_ref, out_ref):
    lane = lax.broadcasted_iota(jnp.int32, (1, ROWS), 1)
    marks = jnp.where(lane < count_ref[0], position_ref[...] + 1, 0)
    spot = lax.broadcasted_iota(jnp.int32, (MARK_ROWS, ROWS), 0)
    coded = jnp.where(spot == 0, marks >> 8, jnp.where(spot == 1, marks & 255, 0))
    coded = coded.astype(f32).astype(bf16)
    for h in range(HEADS):
        out_ref[h, :ROWS, :KD] = key_ref[h]
        out_ref[h, :ROWS, KD:] = value_ref[h]
        out_ref[h, ROWS:, :ROWS] = coded
        out_ref[h, ROWS:, ROWS:] = jnp.zeros((MARK_ROWS, KD + VD - ROWS), bf16)


def pack_heads(query_ref, keys_ref, past_ref, out_ref):
    for h in range(HEADS):
        out_ref[h, :, : KD + VD] = keys_ref[h]
        out_ref[h, :ROWS, KD + VD : BEFORE] = query_ref[h]
        out_ref[h, ROWS:, KD + VD : BEFORE] = jnp.zeros((MARK_ROWS, KD), bf16)
        out_ref[h, :, BEFORE:] = past_ref[h]


def attend(blocks_ref, out_ref):
    row = lax.broadcasted_iota(jnp.int32, (ROWS, ROWS), 0)
    col = lax.broadcasted_iota(jnp.int32, (ROWS, ROWS), 1)

    def marks_of(start, j):
        coded = blocks_ref[j, ROWS : ROWS + MARK_ROWS, start : start + ROWS].astype(f32)
        return coded[0:1, :] * 256.0 + coded[1:2, :]

    marks = [marks_of(0, j) for j in range(4)]
    here_marks = [jnp.where(m > 0.0, m, 1e9) for m in marks]
    past_marks = [marks_of(BEFORE, j) for j in range(4)]
    past_marks = [jnp.where(m > 0.0, m, 1e9) for m in past_marks]
    for j in range(4):
        query_marks = jnp.sum(jnp.where(row == col, marks[j], 0.0), axis=1, keepdims=True)
        q = blocks_ref[j, :ROWS, KD + VD : BEFORE]
        sources = [(0, i, here_marks[i]) for i in range(j + 1)]
        sources += [(BEFORE, i, past_marks[i]) for i in range(j, 4)]
        scores = []
        for start, i, key_marks in sources:
            score = dot(q, blocks_ref[i, :ROWS, start : start + KD], ((1,), (1,))) * KD**-0.5
            allowed = (key_marks <= query_marks) & (key_marks > query_marks - float(WINDOW))
            scores.append(jnp.where(allowed, score, -1e30))
        top = scores[0]
        for score in scores[1:]:
            top = jnp.maximum(top, score)
        top = jnp.max(top, axis=1, keepdims=True)
        weight_sum = jnp.zeros((ROWS, ROWS), f32)
        mixed = jnp.zeros((ROWS, VD), f32)
        for score, (start, i, key_marks) in zip(scores, sources):
            weights = jnp.exp(score - top)
            weight_sum = weight_sum + weights
            values = blocks_ref[i, :ROWS, start + KD : start + KD + VD]
            mixed = mixed + dot(weights.astype(bf16), values)
        mixed = mixed / jnp.sum(weight_sum, axis=1, keepdims=True)
        out_ref[j] = jnp.where(query_marks > 0.0, mixed, 0.0).astype(bf16)


def heads_first(block):
    return jnp.swapaxes(block, 0, 1)


def shape_of(*dims, kind=f32):
    return jax.ShapeDtypeStruct(dims, kind)


def shards(
    delta_query,
    delta_key,
    delta_value,
    delta_gate,
    delta_beta,
    delta_count,
    delta_gain,
    attn_query,
    attn_key,
    attn_value,
    attn_position,
    attn_count,
):
    keys = call(
        pack_keys, shape_of(HEADS, ROWS + MARK_ROWS, KD + VD, kind=bf16), scalars=1, inputs=3
    )(attn_count, heads_first(attn_key), heads_first(attn_value), attn_position.reshape(1, ROWS))
    past = lax.ppermute(keys, ("zh", "zl"), [(i, i + 1) for i in range(15)])
    maps, carry, local = call(
        block_terms,
        (
            shape_of(HEADS, KD, 2 * KD + VD, kind=bf16),
            shape_of(HEADS, ROWS, KD),
            shape_of(HEADS, ROWS, VD),
        ),
        scalars=1,
        inputs=5,
        scratch=[pltpu.VMEM((HEADS, ROWS, ROWS), f32)] * 2,
        flops=8e9,
        mib=16,
    )(
        delta_count,
        heads_first(delta_query),
        heads_first(delta_key),
        heads_first(delta_value),
        delta_gate.T,
        delta_beta.T,
    )
    maps, attn_query = lax.optimization_barrier((maps, attn_query))
    exchanged = lax.all_to_all(maps, "x", 0, 0, tiled=True)
    exchanged, past = lax.optimization_barrier((exchanged, past))
    packed = call(
        pack_heads, shape_of(HEADS, ROWS + MARK_ROWS, BEFORE + KD + VD, kind=bf16), inputs=3
    )(heads_first(attn_query), keys, past)
    plane_prefix, plane_total = call(
        compose_plane, (shape_of(3, KD, KD + VD), shape_of(4, KD + PART, KD))
    )(exchanged)
    gathered = lax.all_to_all(plane_total, "zl", 0, 0, tiled=True)
    group_prefix, group_total, group_offset = call(
        compose_group,
        (shape_of(3, KD, KD + PART), shape_of(KD + PART, KD), shape_of(PART, KD)),
    )(gathered)
    _, packed = lax.optimization_barrier((group_total, packed))
    blocks = lax.all_to_all(packed, "x", 0, 0, tiled=True)
    first = lax.ppermute(group_offset, "zh", [(0, 1)])
    third = lax.ppermute(group_total, "zh", [(2, 3)])
    pair = call(step_state, shape_of(PART, KD), inputs=2)(group_total, first)
    one = lax.ppermute(pair, "zh", [(1, 2)])
    two = lax.ppermute(pair, "zh", [(1, 3)])
    place = lax.axis_index("zh").astype(jnp.int32).reshape(1)
    planes = call(group_states, shape_of(4, PART, KD), scalars=1, inputs=5)(
        place, first, one, two, third, group_prefix
    )
    planes, blocks = lax.optimization_barrier((planes, blocks))
    attn_heads = call(attend, shape_of(4, ROWS, VD, kind=bf16), flops=8e9, mib=16)(blocks)
    parts = lax.all_to_all(planes, "zl", 0, 0, tiled=True)
    returned = call(plane_states, shape_of(4, KD + ROWS, VD, kind=bf16), inputs=3)(
        parts, plane_prefix, attn_heads
    )
    states = lax.all_to_all(returned, "x", 0, 0, tiled=True)
    raw, squares = call(
        raw_rows, (shape_of(HEADS, ROWS, VD), shape_of(64, ROWS)), inputs=3
    )(carry, local, states)
    squares = lax.all_to_all(squares, "head", 0, 0, tiled=True)
    delta_heads = call(normed, shape_of(HEADS, ROWS, VD, kind=bf16), scalars=1, inputs=3)(
        delta_count, raw, squares, delta_gain
    )
    return (heads_first(delta_heads), heads_first(states[:, KD:]))


def solution(mesh):
    grid = Mesh(mesh.devices.reshape(4, 4, 4, 8), SEQ + ("head",))
    rows = P(SEQ, "head", None)
    pairs = P(SEQ, "head")
    block = P(SEQ)
    return jax.shard_map(
        shards,
        mesh=grid,
        in_specs=(rows, rows, rows, pairs, pairs, block, P("head", None), rows, rows, rows, block, block),
        out_specs=(rows, rows),
        check_vma=False,
    )
```

```python
import jax
import jax.numpy as jnp
from jax import lax
from jax.experimental import pallas as pl
from jax.experimental.pallas import tpu as pltpu
from jax.sharding import Mesh, PartitionSpec as P

ROWS = 256
KD = 128
VD = 256
HEADS = 4
HIDDEN = 8192
WINDOW = 2048
PART = VD // 4
MARK_ROWS = 16
BEFORE = 2 * KD + VD

SEQ = ("zh", "zl", "x")
f32 = jnp.float32
bf16 = jnp.bfloat16


def halves(x):
    high = x.astype(bf16)
    return high, (x - high.astype(f32)).astype(bf16)


def dot(a, b, dims=((1,), (0,))):
    return lax.dot_general(a, b, (dims, ((), ())), preferred_element_type=f32)


def dot3(a, b):
    ah, al = halves(a)
    bh, bl = halves(b)
    return dot(ah, bh) + (dot(ah, bl) + dot(al, bh))


def dot2(a, b):
    ah, al = halves(a)
    return dot(ah, b) + dot(al, b)


def call(body, out_shape, scalars=0, inputs=1, scratch=(), flops=1e7, mib=8):
    whole = pl.BlockSpec(memory_space=pltpu.VMEM)
    small = pl.BlockSpec(memory_space=pltpu.SMEM)
    return pl.pallas_call(
        body,
        in_specs=[small] * scalars + [whole] * inputs,
        out_specs=jax.tree.map(lambda _: whole, out_shape),
        out_shape=out_shape,
        scratch_shapes=list(scratch),
        cost_estimate=pl.CostEstimate(flops=int(flops), bytes_accessed=10**6, transcendentals=0),
        compiler_params=pltpu.CompilerParams(vmem_limit_bytes=mib * 2**20),
    )


def block_terms(
    count_ref, q_ref, k_ref, v_ref, gate_ref, beta_ref, map_ref, carry_ref, local_ref, x_ref, a_ref
):
    count = count_ref[0]
    row = lax.broadcasted_iota(jnp.int32, (ROWS, ROWS), 0)
    col = lax.broadcasted_iota(jnp.int32, (ROWS, ROWS), 1)
    lane = lax.broadcasted_iota(jnp.int32, (1, ROWS), 1)
    eye = row == col
    kept = []
    for h in range(HEADS):
        k = k_ref[h]
        gate = jnp.where(lane < count, gate_ref[h : h + 1, :], 0.0)
        beta = jnp.where(lane < count, beta_ref[h : h + 1, :], 0.0)
        log_col = jnp.sum(jnp.where(col <= row, gate, 0.0), axis=1, keepdims=True)
        log_row = jnp.sum(jnp.where(eye, log_col, 0.0), axis=0, keepdims=True)
        beta_col = jnp.sum(jnp.where(eye, beta, 0.0), axis=1, keepdims=True)
        gram = dot(k, k, ((1,), (1,)))
        squares = jnp.where(eye, gram, 0.0)
        k_col = lax.rsqrt(jnp.sum(squares, axis=1, keepdims=True) + 1e-6)
        k_row = lax.rsqrt(jnp.sum(squares, axis=0, keepdims=True) + 1e-6)
        decay = jnp.where(col <= row, jnp.exp(jnp.minimum(log_col - log_row, 0.0)), 0.0)
        a = jnp.where(col < row, (beta_col * k_col) * decay * (gram * k_row), 0.0)
        a_ref[h] = a
        x_ref[h] = jnp.where(eye, 1.0, jnp.where((row >> 1) == (col >> 1), -a, 0.0))
        q = q_ref[h]
        wide = q.astype(f32)
        q_col = lax.rsqrt(jnp.sum(wide * wide, axis=1, keepdims=True) + 1e-6)
        local_ref[h] = (q_col * decay) * (dot(q, k, ((1,), (1,))) * k_row)
        kept.append((log_col, log_row, beta, k_col, k_row, q_col))
    step = 1
    while (2 << step) <= ROWS:
        m = 1 << step
        for h in range(HEADS):
            if m < 64:
                x = x_ref[h]
                below = ((row >> (step + 1)) == (col >> (step + 1))) & ((row >> step) != (col >> step))
                coarse = x.astype(bf16)
                between = jnp.where(below, a_ref[h], 0.0).astype(bf16)
                x_ref[h] = x - dot(dot(coarse, between).astype(bf16), coarse)
            else:
                for s in range(0, ROWS, 2 * m):
                    first = x_ref[h, s : s + m, s : s + m].astype(bf16)
                    second = x_ref[h, s + m : s + 2 * m, s + m : s + 2 * m].astype(bf16)
                    between = a_ref[h, s + m : s + 2 * m, s : s + m].astype(bf16)
                    x_ref[h, s + m : s + 2 * m, s : s + m] = -dot(
                        second, dot(between, first).astype(bf16)
                    )
        step += 1
    for h in range(HEADS):
        x = x_ref[h]
        left = jnp.where(eye, 1.0, 0.0) - x - dot3(a_ref[h], x)
        x_ref[h] = x + dot(x.astype(bf16), left.astype(bf16))
    row_k = lax.broadcasted_iota(jnp.int32, (KD, KD), 0)
    col_k = lax.broadcasted_iota(jnp.int32, (KD, KD), 1)
    for h in range(HEADS):
        log_col, log_row, beta, k_col, k_row, q_col = kept[h]
        k = k_ref[h]
        x = x_ref[h]
        new_value = dot2(x * beta, v_ref[h])
        new_key = dot2(x * (beta * jnp.exp(log_row) * k_row), k)
        new = jnp.concatenate([new_key, new_value], axis=1)
        last = log_col[ROWS - 1 : ROWS, :]
        high, low = halves((jnp.exp(last - log_col) * k_col) * new)
        update = dot(k, high, ((0,), (0,))) + dot(k, low, ((0,), (0,)))
        transition = jnp.where(row_k == col_k, jnp.exp(last), 0.0) - update[:, :KD]
        map_ref[h, :, :KD], map_ref[h, :, KD : 2 * KD] = halves(transition)
        map_ref[h, :, 2 * KD :] = update[:, KD:].astype(bf16)
        mixed = dot3(local_ref[h], new)
        carry_ref[h] = (jnp.exp(log_col) * q_col) * q_ref[h].astype(f32) - mixed[:, :KD]
        local_ref[h] = mixed[:, KD:]


def fold(x):
    half = KD // 2
    return jnp.concatenate([x[:half, :], x[half:, :]], axis=1)


def unfold(x):
    return jnp.concatenate([x[:, :PART], x[:, PART:]], axis=0)


def then(state, transition, offset):
    state = dot3(transition, state)
    return jnp.concatenate([state[:, :KD], state[:, KD:] + offset], axis=1)


def compose_plane(maps_ref, before_ref, send_ref):
    def map_of(i):
        wide = maps_ref[i].astype(f32)
        return wide[:, :KD] + wide[:, KD : 2 * KD], wide[:, 2 * KD :]

    state = jnp.concatenate(map_of(0), axis=1)
    for i in range(1, 4):
        before_ref[i - 1] = state
        state = then(state, *map_of(i))
    for i in range(4):
        send_ref[i, :KD, :] = state[:, :KD]
        send_ref[i, KD:, :] = fold(state[:, KD + i * PART : KD + (i + 1) * PART])


def compose_group(maps_ref, before_ref, total_ref, offset_ref):
    state = jnp.concatenate([maps_ref[0, :KD, :], unfold(maps_ref[0, KD:, :])], axis=1)
    for i in range(1, 4):
        before_ref[i - 1] = state
        state = then(state, maps_ref[i, :KD, :], unfold(maps_ref[i, KD:, :]))
    offset = fold(state[:, KD:])
    total_ref[:KD, :] = state[:, :KD]
    total_ref[KD:, :] = offset
    offset_ref[...] = offset


def step_state(map_ref, earlier_ref, out_ref):
    state = dot3(map_ref[:KD, :], unfold(earlier_ref[...]))
    out_ref[...] = fold(state) + map_ref[KD:, :]


def group_states(place_ref, first_ref, one_ref, two_ref, third_ref, before_ref, out_ref):
    place = place_ref[0]
    last = fold(dot3(third_ref[:KD, :], unfold(two_ref[...]))) + third_ref[KD:, :]
    state = jnp.where(
        place == 0,
        0.0,
        jnp.where(place == 1, first_ref[...], jnp.where(place == 2, one_ref[...], last)),
    )
    out_ref[0] = state
    state = unfold(state)
    for i in range(3):
        out_ref[i + 1] = fold(dot3(before_ref[i, :, :KD], state) + before_ref[i, :, KD:])


def plane_states(parts_ref, before_ref, attn_ref, out_ref):
    state = jnp.concatenate([unfold(parts_ref[i]) for i in range(4)], axis=1)
    for i in range(4):
        entering = state
        if i > 0:
            entering = dot3(before_ref[i - 1, :, :KD], state) + before_ref[i - 1, :, KD:]
        out_ref[i, :KD, :] = entering.astype(bf16)
        out_ref[i, KD:, :] = attn_ref[i]


def raw_rows(carry_ref, local_ref, state_ref, raw_ref, square_ref):
    total = jnp.zeros((ROWS, VD), f32)
    for h in range(HEADS):
        raw = local_ref[h] + dot2(carry_ref[h], state_ref[h, :KD, :])
        raw_ref[h] = raw
        total = total + raw * raw
    column = jnp.sum(total, axis=1, keepdims=True)
    row = lax.broadcasted_iota(jnp.int32, (ROWS, ROWS), 0)
    col = lax.broadcasted_iota(jnp.int32, (ROWS, ROWS), 1)
    square_ref[...] = jnp.broadcast_to(
        jnp.sum(jnp.where(row == col, column, 0.0), axis=0, keepdims=True), square_ref.shape
    )


def normed(count_ref, raw_ref, square_ref, gain_ref, out_ref):
    row = lax.broadcasted_iota(jnp.int32, (ROWS, ROWS), 0)
    col = lax.broadcasted_iota(jnp.int32, (ROWS, ROWS), 1)
    total = square_ref[0:1, :]
    for i in range(1, 8):
        total = total + square_ref[8 * i : 8 * i + 1, :]
    column = jnp.sum(jnp.where(row == col, total, 0.0), axis=1, keepdims=True)
    live = lax.broadcasted_iota(jnp.int32, (ROWS, 1), 0) < count_ref[0]
    factor = jnp.where(live, lax.rsqrt(column * (1.0 / HIDDEN) + 1e-6), 0.0)
    for h in range(HEADS):
        out_ref[h] = (raw_ref[h] * factor * gain_ref[h : h + 1, :]).astype(bf16)


def pack_keys(count_ref, key_ref, value_ref, position_ref, out_ref):
    lane = lax.broadcasted_iota(jnp.int32, (1, ROWS), 1)
    marks = jnp.where(lane < count_ref[0], position_ref[...] + 1, 0)
    spot = lax.broadcasted_iota(jnp.int32, (MARK_ROWS, ROWS), 0)
    coded = jnp.where(spot == 0, marks >> 8, jnp.where(spot == 1, marks & 255, 0))
    coded = coded.astype(f32).astype(bf16)
    for h in range(HEADS):
        out_ref[h, :ROWS, :KD] = key_ref[h]
        out_ref[h, :ROWS, KD:] = value_ref[h]
        out_ref[h, ROWS:, :ROWS] = coded
        out_ref[h, ROWS:, ROWS:] = jnp.zeros((MARK_ROWS, KD + VD - ROWS), bf16)


def pack_heads(query_ref, keys_ref, past_ref, out_ref):
    for h in range(HEADS):
        out_ref[h, :, : KD + VD] = keys_ref[h]
        out_ref[h, :ROWS, KD + VD : BEFORE] = query_ref[h]
        out_ref[h, ROWS:, KD + VD : BEFORE] = jnp.zeros((MARK_ROWS, KD), bf16)
        out_ref[h, :, BEFORE:] = past_ref[h]


def attend(blocks_ref, out_ref):
    row = lax.broadcasted_iota(jnp.int32, (ROWS, ROWS), 0)
    col = lax.broadcasted_iota(jnp.int32, (ROWS, ROWS), 1)

    def marks_of(start, j):
        coded = blocks_ref[j, ROWS : ROWS + MARK_ROWS, start : start + ROWS].astype(f32)
        return coded[0:1, :] * 256.0 + coded[1:2, :]

    marks = [marks_of(0, j) for j in range(4)]
    here_marks = [jnp.where(m > 0.0, m, 1e9) for m in marks]
    past_marks = [marks_of(BEFORE, j) for j in range(4)]
    past_marks = [jnp.where(m > 0.0, m, 1e9) for m in past_marks]
    for j in range(4):
        query_marks = jnp.sum(jnp.where(row == col, marks[j], 0.0), axis=1, keepdims=True)
        q = blocks_ref[j, :ROWS, KD + VD : BEFORE]
        sources = [(0, i, here_marks[i]) for i in range(j + 1)]
        sources += [(BEFORE, i, past_marks[i]) for i in range(j, 4)]
        scores = []
        for start, i, key_marks in sources:
            score = dot(q, blocks_ref[i, :ROWS, start : start + KD], ((1,), (1,))) * KD**-0.5
            allowed = (key_marks <= query_marks) & (key_marks > query_marks - float(WINDOW))
            scores.append(jnp.where(allowed, score, -1e30))
        top = scores[0]
        for score in scores[1:]:
            top = jnp.maximum(top, score)
        top = jnp.max(top, axis=1, keepdims=True)
        weight_sum = jnp.zeros((ROWS, ROWS), f32)
        mixed = jnp.zeros((ROWS, VD), f32)
        for score, (start, i, key_marks) in zip(scores, sources):
            weights = jnp.exp(score - top)
            weight_sum = weight_sum + weights
            values = blocks_ref[i, :ROWS, start + KD : start + KD + VD]
            mixed = mixed + dot(weights.astype(bf16), values)
        mixed = mixed / jnp.sum(weight_sum, axis=1, keepdims=True)
        out_ref[j] = jnp.where(query_marks > 0.0, mixed, 0.0).astype(bf16)


def heads_first(block):
    return jnp.swapaxes(block, 0, 1)


def shape_of(*dims, kind=f32):
    return jax.ShapeDtypeStruct(dims, kind)


def shards(
    delta_query,
    delta_key,
    delta_value,
    delta_gate,
    delta_beta,
    delta_count,
    delta_gain,
    attn_query,
    attn_key,
    attn_value,
    attn_position,
    attn_count,
):
    keys = call(
        pack_keys, shape_of(HEADS, ROWS + MARK_ROWS, KD + VD, kind=bf16), scalars=1, inputs=3
    )(attn_count, heads_first(attn_key), heads_first(attn_value), attn_position.reshape(1, ROWS))
    past = lax.ppermute(keys, ("zh", "zl"), [(i, i + 1) for i in range(15)])
    maps, carry, local = call(
        block_terms,
        (
            shape_of(HEADS, KD, 2 * KD + VD, kind=bf16),
            shape_of(HEADS, ROWS, KD),
            shape_of(HEADS, ROWS, VD),
        ),
        scalars=1,
        inputs=5,
        scratch=[pltpu.VMEM((HEADS, ROWS, ROWS), f32)] * 2,
        flops=8e9,
        mib=16,
    )(
        delta_count,
        heads_first(delta_query),
        heads_first(delta_key),
        heads_first(delta_value),
        delta_gate.T,
        delta_beta.T,
    )
    maps, attn_query = lax.optimization_barrier((maps, attn_query))
    exchanged = lax.all_to_all(maps, "x", 0, 0, tiled=True)
    exchanged, past = lax.optimization_barrier((exchanged, past))
    packed = call(
        pack_heads, shape_of(HEADS, ROWS + MARK_ROWS, BEFORE + KD + VD, kind=bf16), inputs=3
    )(heads_first(attn_query), keys, past)
    plane_prefix, plane_total = call(
        compose_plane, (shape_of(3, KD, KD + VD), shape_of(4, KD + PART, KD))
    )(exchanged)
    gathered = lax.all_to_all(plane_total, "zl", 0, 0, tiled=True)
    group_prefix, group_total, group_offset = call(
        compose_group,
        (shape_of(3, KD, KD + PART), shape_of(KD + PART, KD), shape_of(PART, KD)),
    )(gathered)
    _, packed = lax.optimization_barrier((group_total, packed))
    blocks = lax.all_to_all(packed, "x", 0, 0, tiled=True)
    first = lax.ppermute(group_offset, "zh", [(0, 1)])
    third = lax.ppermute(group_total, "zh", [(2, 3)])
    pair = call(step_state, shape_of(PART, KD), inputs=2)(group_total, first)
    two = lax.ppermute(pair, "zh", [(1, 3)])
    third, pair = lax.optimization_barrier((third, pair))
    one = lax.ppermute(pair, "zh", [(1, 2)])
    place = lax.axis_index("zh").astype(jnp.int32).reshape(1)
    planes = call(group_states, shape_of(4, PART, KD), scalars=1, inputs=5)(
        place, first, one, two, third, group_prefix
    )
    planes, blocks = lax.optimization_barrier((planes, blocks))
    attn_heads = call(attend, shape_of(4, ROWS, VD, kind=bf16), flops=8e9, mib=16)(blocks)
    parts = lax.all_to_all(planes, "zl", 0, 0, tiled=True)
    returned = call(plane_states, shape_of(4, KD + ROWS, VD, kind=bf16), inputs=3)(
        parts, plane_prefix, attn_heads
    )
    states = lax.all_to_all(returned, "x", 0, 0, tiled=True)
    raw, squares = call(
        raw_rows, (shape_of(HEADS, ROWS, VD), shape_of(64, ROWS)), inputs=3
    )(carry, local, states)
    squares = lax.all_to_all(squares, "head", 0, 0, tiled=True)
    delta_heads = call(normed, shape_of(HEADS, ROWS, VD, kind=bf16), scalars=1, inputs=3)(
        delta_count, raw, squares, delta_gain
    )
    return (heads_first(delta_heads), heads_first(states[:, KD:]))


def solution(mesh):
    grid = Mesh(mesh.devices.reshape(4, 4, 4, 8), SEQ + ("head",))
    rows = P(SEQ, "head", None)
    pairs = P(SEQ, "head")
    block = P(SEQ)
    return jax.shard_map(
        shards,
        mesh=grid,
        in_specs=(rows, rows, rows, pairs, pairs, block, P("head", None), rows, rows, rows, block, block),
        out_specs=(rows, rows),
        check_vma=False,
    )
```
